128 devices in a mesh: expert: 32 (over z, x, core), shard: 4 (over y).
Axes of the slice: x: 4, y: 4, z: 4, core: 2. Of those that a mesh axis runs over, the one named last changes fastest.
Arguments:
- hidden_in: bfloat16 [32768, 1024], P(('expert', 'shard')), may hold values from -6 to 6
- seq_lengths: int32 [32, 4], P('expert'), may hold values from 1 to 896, 1024 in all within a row
- routes: int32 [32768, 8], P(('expert', 'shard')), may hold values from 0 to 31, all different within a row; in each aligned block of 256 rows (0 to 255, 256 to 511, ...) at most 96 rows name the same one
- norm_gain1: float32 [1024], replicated, may hold values from 0.5 to 1.5
- w_query: bfloat16 [1024, 1024], P(None, 'shard'), may hold values from -0.1875 to 0.1875
- w_key: bfloat16 [1024, 512], P(None, 'shard'), may hold values from -0.1875 to 0.1875
- w_value: bfloat16 [1024, 512], P(None, 'shard'), may hold values from -0.1875 to 0.1875
- query_gain: float32 [64], replicated, may hold values from 0.5 to 1.5
- key_gain: float32 [64], replicated, may hold values from 0.5 to 1.5
- w_out: bfloat16 [1024, 1024], P('shard'), may hold values from -3 to 3
- norm_gain2: float32 [1024], replicated, may hold values from 0.5 to 1.5
- w_router: bfloat16 [1024, 32], replicated, may hold values from -0.09375 to 0.09375
- w_gate: bfloat16 [32, 1024, 512], P('expert', None, 'shard'), may hold values from -0.1875 to 0.1875
- w_up: bfloat16 [32, 1024, 512], P('expert', None, 'shard'), may hold values from -0.1875 to 0.1875
- w_down: bfloat16 [32, 1024, 512], P('expert', None, 'shard'), may hold values from -4 to 4
- cotangent: bfloat16 [32768, 1024], P(('expert', 'shard')), may hold values from -6 to 6
Outputs:
- hidden_out: bfloat16 [32768, 1024], P(('expert', 'shard'))
- grad_hidden: float32 [32768, 1024], P(('expert', 'shard'))
- grad_norm_gain1: float32 [1024], replicated
- grad_w_query: float32 [1024, 1024], P(None, 'shard')
- grad_w_key: float32 [1024, 512], P(None, 'shard')
- grad_w_value: float32 [1024, 512], P(None, 'shard')
- grad_query_gain: float32 [64], replicated
- grad_key_gain: float32 [64], replicated
- grad_w_out: float32 [1024, 1024], P('shard')
- grad_norm_gain2: float32 [1024], replicated
- grad_w_router: float32 [1024, 32], replicated
- grad_w_gate: float32 [32, 1024, 512], P('expert', None, 'shard')
- grad_w_up: float32 [32, 1024, 512], P('expert', None, 'shard')
- grad_w_down: float32 [32, 1024, 512], P('expert', None, 'shard')
The draws below stay inside these ranges and needn't reach their ends.
Inputs may be any that keep to these rules, and one draw needn't show every extreme that they name: `seq_lengths`: row i lists, in order, the lengths of the 4 sequences packed into the 1024 tokens of index i of expert; each row sums to 1024, and its longest has exactly 896 tokens. `routes`: each row names 8 different experts. In the 256 rows of one device no expert is named more than 96 times; in every draw some expert is named exactly 96 times by the rows of some device.
All inputs are finite; a program needn't handle non-finite values.
Results may differ from the reference program's by a relative error of at most 0.025.
Values may be sent and summed in bfloat16 or wider, within the bound.
No kernel may reach another device: no remote copies, remote signals or barrier semaphores. Data moves between devices by JAX's collectives and lax.ppermute only.
A program may use at most 192 MiB of HBM per device.

```python
import math
from functools import partial
import jax
import jax.numpy as jnp
import numpy as np
from jax import lax

D = 1024
HEADS = 16
KV_HEADS = 8
HEAD_DIM = 64
EXPERTS = 32
TOP = 8
FF = 512
TOK_DEV = 256
SEQS = 4
CAP = 96
GROUP = 1024
TOKENS = 32768
N_EXPERT = 32


def levels(own_key, extent, shards, least, largest):
    gain = 1.0
    for dim, shards_of in shards:
        draws = jax.random.uniform(jax.random.fold_in(jax.random.fold_in(own_key, 6), dim), (shards_of,), jnp.float32, least / len(shards), largest / len(shards))
        gain = gain * jnp.repeat(jnp.exp(draws), extent[dim] // shards_of).reshape((-1,) + (1,) * (len(extent) - 1 - dim))
    return gain


def length_profile(number_of, total, reach, slope):
    weights = [(1 << 20) // math.isqrt(standing ** slope) + 1 for standing in range(2, number_of + 1)]
    rest, given = total - reach - (number_of - 1), [1] * (number_of - 1)
    while rest > 0:
        free = [i for i in range(number_of - 1) if given[i] < reach]
        pool, budget = sum([weights[i] for i in free]), rest
        for i in free:
            extra = min(reach - given[i], max(1, budget * weights[i] // pool), rest)
            given[i] = given[i] + extra
            rest = rest - extra
    return np.array([reach] + given)


def uneven(own_key, amount, total, bound, skew):
    if amount == 2:
        one = jax.random.randint(own_key, (), max(1, total - bound), min(bound, total - 1) + 1)
        return jnp.stack([one, total - one])
    lengths = jnp.asarray(length_profile(amount, total, bound, skew), jnp.int32)
    couples = (amount - 1) // 2
    giver, taker = lengths[1:1 + 2 * couples:2], lengths[2:2 + 2 * couples:2]
    room = jnp.minimum(giver - 1, bound - taker)
    shifted = jax.random.randint(jax.random.fold_in(own_key, 1), (couples,), 0, 1 << 20) % (room + 1)
    lengths = lengths.at[1:1 + 2 * couples:2].set(giver - shifted).at[2:2 + 2 * couples:2].set(taker + shifted)
    return lengths[jax.random.permutation(jax.random.fold_in(own_key, 2), amount)]


def shared_out(rng, own, number, rows, number_of, top, reach, slope):
    order = jax.random.permutation(rng, number_of)
    heavy_load, common = load_shares(number_of, rows * top, reach, slope, True), load_shares(number_of, rows * top, reach, slope, False)
    places = jnp.arange(number_of)

    def named(lengths, offset_by):
        used = int((lengths > 0).sum())
        fixed = max(1, used // 4)
        passed = fixed + (places - fixed + offset_by * (used - fixed)) % max(1, number_of - fixed)
        return jnp.zeros((number_of,), jnp.int32).at[order[jnp.where(places < fixed, places, passed)]].set(jnp.asarray(lengths, jnp.int32))

    lengths = jnp.where(number % 4 == 0, named(heavy_load, number // 4), named(common, number - number // 4 - 1))
    mixed = jax.random.permutation(jax.random.fold_in(own, 3), number_of)
    donor, receiver = mixed[0:number_of // 2 * 2:2], mixed[1:number_of // 2 * 2:2]
    margin = jnp.minimum(lengths[donor] - 1, reach - lengths[receiver]) // 2
    margin = jnp.where((donor == order[0]) | (receiver == order[0]) | (lengths[receiver] == 0), 0, jnp.maximum(margin, 0))
    passed = jax.random.randint(jax.random.fold_in(own, 4), (number_of // 2,), 0, 1 << 20) % (margin + 1)
    lengths = lengths.at[donor].add(-passed).at[receiver].add(passed)
    items = jnp.searchsorted(jnp.cumsum(lengths), jnp.arange(rows * top), side="right").astype(jnp.int32)
    table = items.reshape(top, rows).T
    table = table[jax.random.permutation(jax.random.fold_in(own, 1), rows)]
    offset_by = jax.random.randint(jax.random.fold_in(own, 2), (rows, 1), 0, top)
    return jnp.take_along_axis(table, (jnp.arange(top)[None, :] + offset_by) % top, axis=1)


def load_shares(number_of, total, limit, skew, full):
    portions = [(1 << 20) // math.isqrt(standing ** skew) + 1 for standing in range(1, number_of + 1)]
    largest = limit if full else min(limit, max(-(-total // number_of), total * portions[0] // sum(portions)))
    least = 1 if total - largest >= number_of - 1 else 0
    given, rest = [largest] + [least] * (number_of - 1), total - largest - least * (number_of - 1)
    while rest > 0:
        movable = [i for i in range(1, number_of) if given[i] < largest] or [i for i in range(1, number_of) if given[i] < limit]
        pool, budget = sum([portions[i] for i in movable]), rest
        for i in movable:
            addition = min(limit - given[i], max(1, budget * portions[i] // pool), rest)
            given[i] = given[i] + addition
            rest = rest - addition
    return np.array(given)


def gaussian(own_key, dims, width, most, shards=(), kind=jnp.bfloat16):
    entries = width * jax.random.normal(own_key, dims, jnp.float32)
    if shards:
        entries = entries * levels(own_key, dims, shards, -0.22, 0.18)
    return jnp.clip(entries, -most, most).astype(kind)


def setup_inputs(seed: int = 0) -> dict:
    arg_keys = jax.random.split(jax.random.key(seed), 17)
    hidden_in = gaussian(arg_keys[0], (TOKENS, D), 1.0, 6.0, ((0, 128),))
    seq_lengths = jax.vmap(lambda own: uneven(own, SEQS, GROUP, GROUP - TOK_DEV // 2, 1))(jax.random.split(arg_keys[1], N_EXPERT)).reshape((N_EXPERT, SEQS)).astype(jnp.int32)
    routes_keys = jax.random.split(jax.random.fold_in(arg_keys[2], 1), TOKENS // TOK_DEV)
    routes_turns = jax.random.permutation(jax.random.fold_in(arg_keys[2], 3), TOKENS // TOK_DEV)
    routes = jax.vmap(lambda own, number: shared_out(jax.random.fold_in(arg_keys[2], 2), own, number, TOK_DEV, EXPERTS, TOP, CAP, 1))(routes_keys, routes_turns).reshape((TOKENS, TOP))
    norm_gain1 = jnp.clip(1.0 + 0.1 * jax.random.normal(arg_keys[3], (D,), jnp.float32), 0.5, 1.5)
    w_query = gaussian(arg_keys[4], (D, HEADS * HEAD_DIM), D ** -0.5, 0.1875, ((1, 4),))
    w_key = gaussian(arg_keys[5], (D, KV_HEADS * HEAD_DIM), D ** -0.5, 0.1875, ((1, 4),))
    w_value = gaussian(arg_keys[6], (D, KV_HEADS * HEAD_DIM), D ** -0.5, 0.1875, ((1, 4),))
    query_gain = jnp.clip(1.0 + 0.1 * jax.random.normal(arg_keys[7], (HEAD_DIM,), jnp.float32), 0.5, 1.5)
    key_gain = jnp.clip(1.0 + 0.1 * jax.random.normal(arg_keys[8], (HEAD_DIM,), jnp.float32), 0.5, 1.5)
    w_out = gaussian(arg_keys[9], (HEADS * HEAD_DIM, D), (HEADS * HEAD_DIM // 256) ** -0.5, 3.0, ((0, 4),))
    norm_gain2 = jnp.clip(1.0 + 0.1 * jax.random.normal(arg_keys[10], (D,), jnp.float32), 0.5, 1.5)
    w_router = gaussian(arg_keys[11], (D, EXPERTS), (4 * D) ** -0.5, 0.09375)
    w_gate = gaussian(arg_keys[12], (EXPERTS, D, FF), D ** -0.5, 0.1875, ((0, 32), (2, 4)))
    w_up = gaussian(arg_keys[13], (EXPERTS, D, FF), D ** -0.5, 0.1875, ((0, 32), (2, 4)))
    w_down = gaussian(arg_keys[14], (EXPERTS, D, FF), 2 ** -0.5, 4.0, ((0, 32), (2, 4)))
    cotangent = gaussian(arg_keys[15], (TOKENS, D), 1.0, 6.0, ((0, 128),))
    return {"hidden_in": hidden_in, "seq_lengths": seq_lengths, "routes": routes, "norm_gain1": norm_gain1, "w_query": w_query, "w_key": w_key, "w_value": w_value, "query_gain": query_gain, "key_gain": key_gain, "w_out": w_out, "norm_gain2": norm_gain2, "w_router": w_router, "w_gate": w_gate, "w_up": w_up, "w_down": w_down, "cotangent": cotangent}


EPS_NORM = 1e-05
EPS_HEAD = 1e-06
ROPE_BASE = 10000.0
MASKED = -1e+30

@jax.custom_vjp
def low(v):
    return lax.optimization_barrier(v.astype(jnp.bfloat16)).astype(jnp.float32)

@jax.custom_vjp
def low_back(v):
    return v

def low_keep(v):
    return (low(v), None)

def low_pass(kept, grad):
    return (grad,)

def back_keep(v):
    return (v, None)

def back_low(kept, grad):
    return (low(grad),)
low.defvjp(low_keep, low_pass)
low_back.defvjp(back_keep, back_low)

def matmul(left, right):
    return jnp.dot(left, right, precision=lax.Precision.HIGHEST, preferred_element_type=jnp.float32)

def rms_scale(row_block, gain_row, epsilon):
    return row_block * lax.rsqrt(lax.optimization_barrier(jnp.mean(row_block * row_block, axis=-1, keepdims=True)) + epsilon) * gain_row

def rotary(head_rows, position):
    half_dim = head_rows.shape[-1] // 2
    frequency = ROPE_BASE ** (-2.0 * jnp.arange(half_dim, dtype=jnp.float32) / head_rows.shape[-1])
    angles = position.astype(jnp.float32)[:, None] * frequency[None, :]
    cosine = jnp.cos(angles)[:, None, :]
    sine_part = jnp.sin(angles)[:, None, :]
    first_half = head_rows[..., :half_dim]
    second = head_rows[..., half_dim:]
    return jnp.concatenate([first_half * cosine - second * sine_part, second * cosine + first_half * sine_part], axis=-1)

def head_prep(raw_rows, gain_row, position):
    return rotary(rms_scale(raw_rows, gain_row, EPS_HEAD), position)

def layout(lengths_row, total_rows):
    row_index = jnp.arange(total_rows, dtype=jnp.int32)
    seq_ends = jnp.cumsum(lengths_row).astype(jnp.int32)
    segment = lax.optimization_barrier(jnp.sum((row_index[:, None] >= seq_ends[None, :]).astype(jnp.int32), axis=1))
    seq_starts = seq_ends - lengths_row.astype(jnp.int32)
    picked = segment[:, None] == jnp.arange(lengths_row.shape[0], dtype=jnp.int32)[None, :]
    position = row_index - lax.optimization_barrier(jnp.sum(jnp.where(picked, seq_starts[None, :], 0), axis=1)).astype(jnp.int32)
    return (segment, position)

def slot_tables(route_rows, capacity):
    choices = route_rows.reshape(-1).astype(jnp.int32)
    onehot = (choices[:, None] == jnp.arange(EXPERTS, dtype=jnp.int32)[None, :]).astype(jnp.int32)
    earlier = jnp.cumsum(onehot, axis=0) - onehot
    ranked = lax.optimization_barrier(jnp.sum(earlier * onehot, axis=1)).astype(jnp.int32)
    slot_of = choices * capacity + ranked
    slot_choice = jnp.full((EXPERTS * capacity,), -1, jnp.int32).at[slot_of].set(jnp.arange(choices.shape[0], dtype=jnp.int32))
    return (slot_of, slot_choice)

def forward(hidden, norm_gain1, w_query, w_key, w_value, query_gain, key_gain, w_out, norm_gain2, w_router, w_gate, w_up, w_down, seq_lengths, routes, slot_of, slot_choice):
    groups = seq_lengths.shape[0]
    group_rows = hidden.shape[0] // groups
    scale = HEAD_DIM ** (-0.5)
    normed = low(rms_scale(hidden, norm_gain1, EPS_NORM))

    def attend(block):
        row_block, lengths_row = block
        segment, position = layout(lengths_row, group_rows)
        q_raw = low_back(matmul(row_block, w_query)).reshape(group_rows, HEADS, HEAD_DIM)
        k_raw = low_back(matmul(row_block, w_key)).reshape(group_rows, KV_HEADS, HEAD_DIM)
        values = low_back(low(matmul(row_block, w_value))).reshape(group_rows, KV_HEADS, HEAD_DIM)
        queries = low(head_prep(q_raw, query_gain, position)).reshape(group_rows, KV_HEADS, HEADS // KV_HEADS, HEAD_DIM)
        keys = low(head_prep(k_raw, key_gain, position))
        scores = low_back(jnp.einsum('qgrd,kgd->grqk', queries, keys, precision=lax.Precision.HIGHEST) * scale)
        same_seq = segment[:, None] == segment[None, :]
        weights = low(jax.nn.softmax(jnp.where(same_seq, scores, MASKED), axis=-1))
        mixed = jnp.einsum('grqk,kgd->qgrd', weights, values, precision=lax.Precision.HIGHEST)
        mixed = low_back(low(mixed)).reshape(group_rows, HEADS * HEAD_DIM)
        return low_back(matmul(mixed, w_out))
    attended = lax.map(jax.checkpoint(attend), (normed.reshape(groups, group_rows, -1), seq_lengths)).reshape(hidden.shape)
    residual = hidden + attended
    normed2 = low(rms_scale(residual, norm_gain2, EPS_NORM))
    logits = low_back(matmul(normed2, w_router))
    router_probs = jax.nn.softmax(logits, axis=-1)
    gate_values = jnp.take_along_axis(router_probs, routes, axis=1)
    blocks = hidden.shape[0] // TOK_DEV

    def expert_block(block):
        row_block, gate_rows, slot_row, choice_row = block
        slot_used = choice_row >= 0
        slot_token = jnp.maximum(choice_row, 0) // TOP
        picked = low_back(jnp.where(slot_used[:, None], row_block[slot_token], 0.0)).reshape(EXPERTS, CAP, -1)
        gate_part = low_back(jnp.einsum('ecd,edf->ecf', picked, w_gate, precision=lax.Precision.HIGHEST))
        up_part = low_back(jnp.einsum('ecd,edf->ecf', picked, w_up, precision=lax.Precision.HIGHEST))
        inner = low(jax.nn.silu(gate_part) * up_part)
        result = jnp.einsum('ecf,edf->ecd', inner, w_down, precision=lax.Precision.HIGHEST)
        result = low_back(low(result)).reshape(EXPERTS * CAP, -1)
        chosen = result[slot_row].reshape(TOK_DEV, TOP, -1)
        return lax.optimization_barrier(jnp.sum(gate_rows[:, :, None] * chosen, axis=1))
    mixture = lax.map(jax.checkpoint(expert_block), (normed2.reshape(blocks, TOK_DEV, -1), gate_values.reshape(blocks, TOK_DEV, TOP), slot_of, slot_choice)).reshape(hidden.shape)
    return residual + mixture

def reference(hidden_in, seq_lengths, routes, norm_gain1, w_query, w_key, w_value, query_gain, key_gain, w_out, norm_gain2, w_router, w_gate, w_up, w_down, cotangent):
    slot_of, slot_choice = jax.vmap(partial(slot_tables, capacity=CAP))(routes.reshape(-1, TOK_DEV, TOP))
    floats = tuple((array_in.astype(jnp.float32) for array_in in (hidden_in, norm_gain1, w_query, w_key, w_value, query_gain, key_gain, w_out, norm_gain2, w_router, w_gate, w_up, w_down)))

    def closed(*params):
        return forward(*params, seq_lengths, routes, slot_of, slot_choice)
    result, pull = jax.vjp(closed, *floats)
    grads = pull(cotangent.astype(jnp.float32))
    return (result.astype(jnp.bfloat16), grads[0], grads[1], grads[2], grads[3], grads[4], grads[5], grads[6], grads[7], grads[8], grads[9], grads[10], grads[11], grads[12])
```

```python
import functools

import jax
import jax.numpy as jnp
from jax import lax
from jax.experimental import pallas as pl
from jax.experimental.pallas import tpu as pltpu
from jax.sharding import PartitionSpec as P

EXPERTS = 32
TOP = 8
CAP = 96
HEAD = 64
HALF = HEAD // 2
SHARDS = 4
GROUP = 1024
WIDTH = 1024
FF = 512

EPS_NORM = 1e-05
EPS_HEAD = 1e-06
ROPE_BASE = 10000.0
APART = 1024.0
MIB = 1 << 20
PIECE = FF // SHARDS

F32 = jnp.float32
BF16 = jnp.bfloat16
EXACT = lax.Precision.HIGHEST


def dot(left, right):
    return jnp.dot(left, right, preferred_element_type=F32)


def dot_nt(left, right):
    return lax.dot_general(left, right, (((1,), (1,)), ((), ())), preferred_element_type=F32)


def dot_tn(left, right):
    return lax.dot_general(left, right, (((0,), (0,)), ((), ())), preferred_element_type=F32)


def fixed(shape):
    zeros = (0,) * len(shape)
    return pl.BlockSpec(shape, lambda *_: zeros, pipeline_mode=pl.Buffered(1))


def params(mebibytes=60):
    return pltpu.CompilerParams(
        dimension_semantics=("arbitrary",), vmem_limit_bytes=mebibytes * MIB
    )


def cost(flops, moved):
    return pl.CostEstimate(flops=int(flops), bytes_accessed=int(moved), transcendentals=0)


def earlier_rows(named):
    tokens = named.shape[1]
    earlier = lax.broadcasted_iota(jnp.int32, (tokens, tokens), 0)
    later = lax.broadcasted_iota(jnp.int32, (tokens, tokens), 1)
    return dot(named.astype(BF16), jnp.where(earlier < later, 1.0, 0.0).astype(BF16))


def rank_table(routes_t):
    tokens = routes_t.shape[1]
    expert = lax.broadcasted_iota(jnp.int32, (EXPERTS, tokens), 0)
    named = jnp.zeros((EXPERTS, tokens), F32)
    for choice in range(TOP):
        named = named + jnp.where(routes_t[choice : choice + 1, :] == expert, 1.0, 0.0)
    return jnp.where(named > 0.5, earlier_rows(named), -1.0).astype(jnp.int32)


def picks(rank, first, slots):
    experts, tokens = rank.shape
    place = lax.broadcasted_iota(jnp.int32, (experts, slots, tokens), 1) + first
    hit = jnp.where(place == rank[:, None, :], 1.0, 0.0).astype(BF16)
    return hit.reshape(experts * slots, tokens)


TOKENS = GROUP // SHARDS
HALF_ROWS = TOKENS // 2
STEP_EXPERTS = 8
STEPS = EXPERTS // STEP_EXPERTS


SOURCES = 8
E_MIB = 60
ROUTE_LANES = TOKENS


def collect_kernel(mine_ref, all_ref, out_ref, rank_ref):
    named = []
    for source in range(SOURCES):
        routes = all_ref[source, TOKENS : TOKENS + TOP, :ROUTE_LANES].astype(F32)
        hits = jnp.where(routes == mine_ref[0].astype(F32), 1.0, 0.0)
        named.append(jnp.sum(hits, axis=0, keepdims=True))
    named = jnp.concatenate(named, axis=0)
    rank = jnp.where(named > 0.5, earlier_rows(named), -1.0).astype(jnp.int32)
    rank_ref[...] = rank
    for source in range(SOURCES):
        pick = picks(rank[source : source + 1, :], 0, CAP)
        out_ref[source] = dot(pick, all_ref[source, :TOKENS, :]).astype(BF16)


def collect(mine, gathered):
    rows = gathered.shape[1]
    return pl.pallas_call(
        collect_kernel,
        grid=(EXPERTS // SOURCES,),
        in_specs=[
            pl.BlockSpec(memory_space=pltpu.SMEM),
            pl.BlockSpec((SOURCES, rows, WIDTH), lambda i: (i, 0, 0)),
        ],
        out_specs=[
            pl.BlockSpec((SOURCES, CAP, WIDTH), lambda i: (i, 0, 0)),
            pl.BlockSpec((SOURCES, TOKENS), lambda i: (i, 0)),
        ],
        out_shape=[
            jax.ShapeDtypeStruct((EXPERTS, CAP, WIDTH), BF16),
            jax.ShapeDtypeStruct((EXPERTS, TOKENS), jnp.int32),
        ],
        compiler_params=params(),
        cost_estimate=cost(2 * EXPERTS * CAP * TOKENS * WIDTH, 24 * MIB),
        name="collect",
    )(mine, gathered)


PARTS = (48, 48)


def slots_kernel(routes_ref, *refs):
    rank = rank_table(routes_ref[...])
    first = 0
    for part, slots in enumerate(PARTS):
        pick = picks(rank, first, slots)
        refs[2 * part][...] = pick
        refs[2 * part + 1][...] = pick.T
        first += slots


def slot_tables(routes_t):
    shapes = []
    for slots in PARTS:
        shapes += [(EXPERTS * slots, TOKENS), (TOKENS, EXPERTS * slots)]
    return pl.pallas_call(
        slots_kernel,
        grid=(1,),
        in_specs=[fixed(routes_t.shape)],
        out_specs=[fixed(shape) for shape in shapes],
        out_shape=[jax.ShapeDtypeStruct(shape, BF16) for shape in shapes],
        compiler_params=params(),
        cost_estimate=cost(0, 4 * MIB),
        name="slot_tables",
    )(routes_t)


def joined_sum(own_ref, from_left, from_right):
    halves = []
    rows = own_ref.shape[0] // 2
    for half in range(2):
        span = slice(half * rows, (half + 1) * rows)
        halves.append(
            own_ref[span, :].astype(F32)
            + from_left[half][...].astype(F32)
            + from_right[half][...].astype(F32)
        )
    return jnp.concatenate(halves, axis=0)


def norm2_kernel(hidden_ref, own_ref, lt_ref, lb_ref, rt_ref, rb_ref, gain_ref, *refs):
    pick_ref, res_ref, rows_ref, out_ref = refs

    @pl.when(pl.program_id(0) == 0)
    def _():
        attended = joined_sum(own_ref, (lt_ref, lb_ref), (rt_ref, rb_ref))
        residual = hidden_ref[...].astype(F32) + attended
        res_ref[...] = residual
        scale = lax.rsqrt(jnp.mean(residual * residual, axis=-1, keepdims=True) + EPS_NORM)
        rows_ref[...] = (residual * scale * gain_ref[...]).astype(BF16)

    out_ref[...] = dot(pick_ref[...], rows_ref[...]).astype(BF16).reshape(out_ref.shape)


def dispatch_kernel(pick_ref, rows_ref, out_ref):
    out_ref[...] = dot(pick_ref[...], rows_ref[...]).astype(BF16).reshape(out_ref.shape)


def dispatch(rows, pick):
    slots = pick.shape[0] // EXPERTS
    tokens = rows.shape[0]
    return pl.pallas_call(
        dispatch_kernel,
        grid=(STEPS,),
        in_specs=[
            pl.BlockSpec((STEP_EXPERTS * slots, tokens), lambda i: (i, 0)),
            fixed(rows.shape),
        ],
        out_specs=pl.BlockSpec((STEP_EXPERTS, slots, WIDTH), lambda i: (i, 0, 0)),
        out_shape=jax.ShapeDtypeStruct((EXPERTS, slots, WIDTH), BF16),
        compiler_params=params(),
        cost_estimate=cost(2 * EXPERTS * slots * tokens * WIDTH, 2 * EXPERTS * slots * WIDTH),
        name="dispatch",
    )(pick, rows)


def norm2_dispatch(hidden, attended, gain, pick):
    whole = (hidden, *attended, gain)
    tokens = hidden.shape[0]
    slots = pick.shape[0] // EXPERTS
    return pl.pallas_call(
        norm2_kernel,
        grid=(STEPS,),
        in_specs=[fixed(array.shape) for array in whole]
        + [pl.BlockSpec((STEP_EXPERTS * slots, tokens), lambda i: (i, 0))],
        out_specs=[
            fixed((tokens, WIDTH)),
            fixed((tokens, WIDTH)),
            pl.BlockSpec((STEP_EXPERTS, slots, WIDTH), lambda i: (i, 0, 0)),
        ],
        out_shape=[
            jax.ShapeDtypeStruct((tokens, WIDTH), F32),
            jax.ShapeDtypeStruct((tokens, WIDTH), BF16),
            jax.ShapeDtypeStruct((EXPERTS, slots, WIDTH), BF16),
        ],
        compiler_params=params(),
        cost_estimate=cost(2 * EXPERTS * slots * tokens * WIDTH, 2 * EXPERTS * slots * WIDTH),
        name="norm2_dispatch",
    )(*whole, pick)


def norm_back(rows, gain, grad):
    scale = lax.rsqrt(jnp.mean(rows * rows, axis=-1, keepdims=True) + EPS_NORM)
    scaled = grad * gain
    inner = jnp.mean(scaled * rows, axis=-1, keepdims=True)
    return scale * scaled - rows * (scale * scale * scale * inner), grad * rows * scale


def norm2_back_kernel(res_ref, gain_ref, cot_ref, *refs):
    place_refs, part_refs = refs[: len(PARTS)], refs[len(PARTS) : 2 * len(PARTS)]
    grad_ref, top_ref, bottom_ref, share_ref, total_ref = refs[2 * len(PARTS) :]
    step = pl.program_id(0)
    total = jnp.zeros(total_ref.shape, F32)
    for place_ref, part_ref, slots in zip(place_refs, part_refs, PARTS):
        total += dot(place_ref[...], part_ref[...].reshape(STEP_EXPERTS * slots, WIDTH))

    @pl.when(step == 0)
    def _():
        total_ref[...] = total

    @pl.when(step > 0)
    def _():
        total_ref[...] += total

    @pl.when(step == STEPS - 1)
    def _():
        back, share = norm_back(res_ref[...], gain_ref[...], total_ref[...])
        grad = cot_ref[...].astype(F32) + back
        grad_ref[...] = grad
        top_ref[...] = grad[:HALF_ROWS].astype(BF16)
        bottom_ref[...] = grad[HALF_ROWS:].astype(BF16)
        share_ref[...] = jnp.sum(share, axis=0, keepdims=True)


def norm2_back(residual, gain, cotangent, places, parts):
    whole = (residual, gain, cotangent)
    tokens = residual.shape[0]
    return pl.pallas_call(
        norm2_back_kernel,
        grid=(STEPS,),
        in_specs=[fixed(array.shape) for array in whole]
        + [pl.BlockSpec((tokens, STEP_EXPERTS * slots), lambda i: (0, i)) for slots in PARTS]
        + [pl.BlockSpec((STEP_EXPERTS, slots, WIDTH), lambda i: (i, 0, 0)) for slots in PARTS],
        out_specs=[
            fixed((tokens, WIDTH)),
            fixed((HALF_ROWS, WIDTH)),
            fixed((HALF_ROWS, WIDTH)),
            fixed((1, WIDTH)),
        ],
        out_shape=[
            jax.ShapeDtypeStruct((tokens, WIDTH), F32),
            jax.ShapeDtypeStruct((HALF_ROWS, WIDTH), BF16),
            jax.ShapeDtypeStruct((HALF_ROWS, WIDTH), BF16),
            jax.ShapeDtypeStruct((1, WIDTH), F32),
        ],
        scratch_shapes=[pltpu.VMEM((tokens, WIDTH), F32)],
        compiler_params=params(24),
        cost_estimate=cost(2 * EXPERTS * CAP * tokens * WIDTH, 2 * EXPERTS * CAP * WIDTH),
        name="norm2_back",
    )(*whole, *places, *parts)


ROW_STEP = 256
ROW_STEPS = GROUP // ROW_STEP
Q_LANES = 256
K_LANES = 128
QK = Q_LANES + K_LANES
QKV = QK + K_LANES
CHIPS = EXPERTS // 2
ROWS_QKV = WIDTH // EXPERTS
ROWS_OUT = Q_LANES // EXPERTS
Q_HEADS = Q_LANES // HEAD
K_HEADS = K_LANES // HEAD
RATIO = Q_HEADS // K_HEADS
LSE_LANE = HEAD + 4


def head_mean(values):
    lanes = values.shape[1]
    row = lax.broadcasted_iota(jnp.int32, (lanes, lanes), 0) // HEAD
    column = lax.broadcasted_iota(jnp.int32, (lanes, lanes), 1) // HEAD
    share = jnp.where(row == column, 1.0 / HEAD, 0.0).astype(F32)
    return jnp.dot(values, share, preferred_element_type=F32, precision=EXACT)


def partner(values):
    lanes = values.shape[1]
    ahead = pltpu.roll(values, lanes - HALF, 1)
    behind = pltpu.roll(values, HALF, 1)
    lane = lax.broadcasted_iota(jnp.int32, values.shape, 1)
    return jnp.where(lane % HEAD < HALF, ahead, behind)


def choose(step, pieces, block_ref):
    for place in range(SHARDS):
        refs = pieces[2 * place : 2 * place + 2]

        @pl.when(step == place)
        def _(refs=refs):
            first = 0
            for ref in refs:
                block_ref[first : first + ref.shape[0], :] = ref[...]
                first += ref.shape[0]


def prep_block(rows, step, gain_ref, w_refs, head_gain_ref, cos_ref, sin_ref, fq_ref, fk_ref, refs):
    normed_ref, raw_q_ref, raw_k_ref, q_ref, k_ref, v_ref = refs
    hidden = rows.astype(F32)
    scale = lax.rsqrt(jnp.mean(hidden * hidden, axis=-1, keepdims=True) + EPS_NORM)
    normed = (hidden * scale * gain_ref[...]).astype(BF16)
    normed_ref[...] = normed
    all_three = jnp.concatenate([dot(normed, w_ref[...]) for w_ref in w_refs], axis=1)
    raw = all_three[:, :QK]
    raw_q_ref[...] = raw[:, :Q_LANES]
    raw_k_ref[...] = raw[:, Q_LANES:]
    scaled = raw * lax.rsqrt(head_mean(raw * raw) + EPS_HEAD) * head_gain_ref[...]
    cosine = jnp.concatenate([cos_ref[...]] * 3, axis=1)
    sine = jnp.concatenate([sin_ref[...]] * 3, axis=1)
    turned = scaled * cosine + partner(scaled) * sine
    span = pl.ds(pl.multiple_of(step * ROW_STEP, ROW_STEP), ROW_STEP)
    for head in range(Q_HEADS):
        part = turned[:, head * HEAD : (head + 1) * HEAD].astype(BF16)
        q_ref[head, span, :] = jnp.concatenate([part * BF16(HEAD**-0.5), fq_ref[...]], axis=1)
    for head in range(K_HEADS):
        first = Q_LANES + head * HEAD
        part = turned[:, first : first + HEAD].astype(BF16)
        k_ref[head, span, :] = jnp.concatenate([part, fk_ref[...]], axis=1)
        value = all_three[:, QK + head * HEAD : QK + (head + 1) * HEAD].astype(BF16)
        v_ref[head, span, :] = jnp.concatenate([value, jnp.ones_like(value)], axis=1)


def attention_kernel(
    h0_ref, h1_ref, h2_ref, h3_ref, h4_ref, h5_ref, h6_ref, h7_ref, gain_ref,
    wq_ref, wk_ref, wv_ref, head_gain_ref, w_out_ref, cos_ref, sin_ref, fq_ref, fk_ref,
    normed_ref, raw_q_ref, raw_k_ref, k_ref, v_ref, mixed_ref, q2_ref, *refs,
):
    out_refs, (block_ref, q_ref) = refs[:-2], refs[-2:]
    step = pl.program_id(0)

    @pl.when(step < ROW_STEPS)
    def _():
        pieces = (h0_ref, h1_ref, h2_ref, h3_ref, h4_ref, h5_ref, h6_ref, h7_ref)
        choose(step, pieces, block_ref)
        prep_block(
            block_ref[...], step, gain_ref, (wq_ref, wk_ref, wv_ref), head_gain_ref, cos_ref, sin_ref, fq_ref, fk_ref,
            (normed_ref, raw_q_ref, raw_k_ref, q_ref, k_ref, v_ref),
        )

    @pl.when(step >= ROW_STEPS)
    def _():
        attend_block(
            step - ROW_STEPS, q_ref, k_ref, v_ref, w_out_ref, mixed_ref, q2_ref, out_refs
        )


def rows_spec(lanes):
    return pl.BlockSpec((ROW_STEP, lanes), lambda i: (i, 0))


def heads_spec(heads):
    return pl.BlockSpec((heads, ROW_STEP, 2 * HEAD), lambda i: (0, i, 0))


PLACES = (
    ((0, TOKENS),),
    ((0, HALF_ROWS), (HALF_ROWS, TOKENS)),
    ((0, HALF_ROWS), (HALF_ROWS, TOKENS)),
    ((0, HALF_ROWS), (HALF_ROWS, TOKENS)),
)
PIECES = [last - first for place in PLACES for first, last in place]


def store_pieces(place, rows, out_refs):
    before = sum(len(spans) for spans in PLACES[:place])
    for ref, (first, last) in zip(out_refs[before:], PLACES[place]):
        ref[...] = rows[first:last]


def attend_block(step, q_ref, k_ref, v_ref, w_ref, mixed_ref, q2_ref, out_refs):
    span = pl.ds(pl.multiple_of(step * ROW_STEP, ROW_STEP), ROW_STEP)
    lane = lax.broadcasted_iota(jnp.int32, (RATIO * ROW_STEP, 2 * HEAD), 1)
    heads = []
    for group in range(K_HEADS):
        queries = q_ref[group * RATIO : (group + 1) * RATIO, span, :]
        queries = queries.reshape(RATIO * ROW_STEP, 2 * HEAD)
        scores = dot_nt(queries, k_ref[group])
        weights = jnp.exp(scores).astype(BF16)
        summed = dot(weights, v_ref[group])
        total = summed[:, HEAD : HEAD + 1]
        mixed = (summed[:, :HEAD] / total).astype(BF16)
        less = -jnp.log(total)
        high = less.astype(BF16).astype(F32)
        middle = (less - high).astype(BF16).astype(F32)
        low = less - high - middle
        extra = jnp.where(
            lane == LSE_LANE,
            high,
            jnp.where(lane == LSE_LANE + 1, middle, jnp.where(lane == LSE_LANE + 2, low, 0.0)),
        )
        q2_ref[group * RATIO : (group + 1) * RATIO] = (
            (queries.astype(F32) + extra).astype(BF16).reshape(RATIO, ROW_STEP, 2 * HEAD)
        )
        for head in range(RATIO):
            heads.append(mixed[head * ROW_STEP : (head + 1) * ROW_STEP])
    joined = jnp.concatenate(heads, axis=1)
    mixed_ref[...] = joined
    rows = dot(joined, w_ref[...]).astype(BF16)
    for place in range(SHARDS):

        @pl.when(step == place)
        def _(place=place):
            store_pieces(place, rows, out_refs)


def early_rows(lanes):
    return pl.BlockSpec((ROW_STEP, lanes), lambda i: (jnp.minimum(i, ROW_STEPS - 1), 0))


def late_rows(lanes):
    return pl.BlockSpec((ROW_STEP, lanes), lambda i: (jnp.maximum(i - ROW_STEPS, 0), 0))


def attention(hidden, gain, weights, head_gain, w_out, cosine, sine, feature_q, feature_k):
    whole = (*hidden, gain, *weights, head_gain, w_out)
    kept = (K_HEADS, GROUP, 2 * HEAD)
    return pl.pallas_call(
        attention_kernel,
        grid=(2 * ROW_STEPS,),
        in_specs=[fixed(array.shape) for array in whole]
        + [early_rows(2 * HEAD), early_rows(2 * HEAD), early_rows(HEAD), early_rows(HEAD)],
        out_specs=[
            early_rows(WIDTH), early_rows(Q_LANES), early_rows(K_LANES), fixed(kept), fixed(kept),
            late_rows(Q_LANES),
            pl.BlockSpec(
                (Q_HEADS, ROW_STEP, 2 * HEAD), lambda i: (0, jnp.maximum(i - ROW_STEPS, 0), 0)
            ),
        ]
        + [fixed((rows, WIDTH)) for rows in PIECES],
        out_shape=[
            jax.ShapeDtypeStruct((GROUP, WIDTH), BF16),
            jax.ShapeDtypeStruct((GROUP, Q_LANES), F32),
            jax.ShapeDtypeStruct((GROUP, K_LANES), F32),
            jax.ShapeDtypeStruct(kept, BF16),
            jax.ShapeDtypeStruct(kept, BF16),
            jax.ShapeDtypeStruct((GROUP, Q_LANES), BF16),
            jax.ShapeDtypeStruct((Q_HEADS, GROUP, 2 * HEAD), BF16),
        ]
        + [jax.ShapeDtypeStruct((rows, WIDTH), BF16) for rows in PIECES],
        scratch_shapes=[
            pltpu.VMEM((TOKENS, WIDTH), BF16),
            pltpu.VMEM((Q_HEADS, GROUP, 2 * HEAD), BF16),
        ],
        compiler_params=params(),
        cost_estimate=cost(Q_HEADS * GROUP * GROUP * 2 * 512 + 2 * GROUP * WIDTH * 512, 16 * MIB),
        name="attention",
    )(*whole, cosine, sine, feature_q, feature_k)


def turn_back(grad, raw, gain, cosine, sine):
    grad = grad * cosine - partner(grad) * sine
    scale = lax.rsqrt(head_mean(raw * raw) + EPS_HEAD)
    scaled = grad * gain
    inner = head_mean(scaled * raw)
    back = scale * scaled - raw * (scale * scale * scale * inner)
    return back, jnp.sum(grad * raw * scale, axis=0, keepdims=True)


def attend_back_kernel(
    core_ref, h0_ref, h1_ref, h2_ref, h3_ref, h4_ref, h5_ref, h6_ref, h7_ref,
    normed_ref, normed_t_ref, gain1_ref, w_qkv_ref, w_ref, q2_ref, k_ref, v_ref, mixed_ref, raw_q_ref, raw_k_ref, gain_ref,
    cos_ref, sin_ref, cos_k_ref, sin_k_ref,
    kept_ref, given_ref, share_ref, share1_ref, *refs,
):
    out_refs, refs = refs[:-7], refs[-7:]
    grad_ref, kt_ref, dk_ref, dv_ref, d_out_acc, d_qkv_ref, load_ref = refs
    step = pl.program_id(0)
    choose(step, (h0_ref, h1_ref, h2_ref, h3_ref, h4_ref, h5_ref, h6_ref, h7_ref), grad_ref)

    @pl.when(step == 0)
    def _():
        for group in range(K_HEADS):
            kt_ref[group] = k_ref[group].T
        dk_ref[...] = jnp.zeros_like(dk_ref)
        dv_ref[...] = jnp.zeros_like(dv_ref)
        share_ref[...] = jnp.zeros_like(share_ref)
        d_out_acc[...] = jnp.zeros_like(d_out_acc)

    d_out_acc[...] += dot_tn(mixed_ref[...], grad_ref[...])
    d_mixed = dot_nt(grad_ref[...], w_ref[...]).astype(BF16)
    wide = d_mixed.astype(F32)
    product = wide * mixed_ref[...].astype(F32)
    lane = lax.broadcasted_iota(jnp.int32, (ROW_STEP, HEAD), 1)
    heads = []
    for head in range(Q_HEADS):
        span = slice(head * HEAD, (head + 1) * HEAD)
        less = -jnp.sum(product[:, span], axis=1, keepdims=True)
        high = less.astype(BF16).astype(F32)
        middle = (less - high).astype(BF16).astype(F32)
        low = less - high - middle
        extra = jnp.where(
            lane == 0, high, jnp.where(lane == 1, middle, jnp.where(lane == 2, low, 0.0))
        )
        heads.append(jnp.concatenate([wide[:, span], extra], axis=1).astype(BF16))
    d_queries = []
    for group in range(K_HEADS):
        queries = q2_ref[group * RATIO : (group + 1) * RATIO].reshape(RATIO * ROW_STEP, 2 * HEAD)
        grads = jnp.concatenate(heads[group * RATIO : (group + 1) * RATIO], axis=0)
        probs = jnp.exp(dot_nt(k_ref[group], queries))
        d_scores = (probs * dot_nt(v_ref[group], grads)).astype(BF16)
        dv_ref[group] += dot(probs.astype(BF16), grads)
        dk_ref[group] += dot(d_scores, queries)
        turned = dot(kt_ref[group], d_scores)[:HEAD].T * (HEAD**-0.5)
        for head in range(RATIO):
            d_queries.append(turned[head * ROW_STEP : (head + 1) * ROW_STEP])
    cosine, sine = cos_ref[...], sin_ref[...]
    back, share = turn_back(
        jnp.concatenate(d_queries, axis=1),
        raw_q_ref[...],
        gain_ref[:, :Q_LANES],
        jnp.concatenate([cosine, cosine], axis=1),
        jnp.concatenate([sine, sine], axis=1),
    )
    d_qkv_ref[pl.ds(pl.multiple_of(step * ROW_STEP, ROW_STEP), ROW_STEP), :Q_LANES] = back.astype(BF16)
    share_ref[:, :Q_LANES] += share

    @pl.when(step == ROW_STEPS - 1)
    def _():
        d_keys = jnp.concatenate([dk_ref[group][:, :HEAD] for group in range(K_HEADS)], axis=1)
        back_k, share_k = turn_back(
            d_keys, raw_k_ref[...], gain_ref[:, Q_LANES:], cos_k_ref[...], sin_k_ref[...]
        )
        d_values = jnp.concatenate([dv_ref[group][:, :HEAD] for group in range(K_HEADS)], axis=1)
        d_qkv_ref[:, Q_LANES:] = jnp.concatenate([back_k, d_values], axis=1).astype(BF16)
        share_ref[:, Q_LANES:] = share_k
        d_w = dot(normed_t_ref[...], d_qkv_ref[...]).astype(BF16)
        load_ref[:, :, :ROWS_QKV] = d_w.reshape(2, CHIPS, ROWS_QKV, QKV)
        d_out = d_out_acc[...].reshape(EXPERTS, ROWS_OUT, WIDTH)
        d_out = jnp.concatenate([d_out[:, :, :QKV], d_out[:, :, QKV:]], axis=1).astype(BF16)
        load_ref[:, :, ROWS_QKV:] = d_out.reshape(2, CHIPS, 2 * ROWS_OUT, QKV)
        kept_ref[...] = load_ref[core_ref[0]]
        given_ref[...] = load_ref[1 - core_ref[0]]
        share1 = jnp.zeros((1, WIDTH), F32)
        for place in range(SHARDS):
            span = slice(place * TOKENS, (place + 1) * TOKENS)
            d_normed = dot_nt(d_qkv_ref[span, :], w_qkv_ref[...])
            store_pieces(place, d_normed.astype(BF16), out_refs)
            share1 += jnp.sum(d_normed * normed_ref[span, :].astype(F32), axis=0, keepdims=True)
        share1_ref[...] = share1 / gain1_ref[...]


def attend_back(
    core, grads, normed, normed_t, gain1, w_qkv, w_out, queries, keys, values, mixed, raw_q, raw_k, head_gain,
    cosine, sine,
):
    load = (CHIPS, ROWS_QKV + 2 * ROWS_OUT, QKV)
    return pl.pallas_call(
        attend_back_kernel,
        grid=(ROW_STEPS,),
        in_specs=[
            pl.BlockSpec(memory_space=pltpu.SMEM),
            *[fixed(piece.shape) for piece in grads],
            fixed(normed.shape), fixed(normed_t.shape), fixed(gain1.shape), fixed(w_qkv.shape),
            fixed(w_out.shape), heads_spec(Q_HEADS), fixed(keys.shape),
            fixed(values.shape), rows_spec(Q_LANES), rows_spec(Q_LANES), fixed(raw_k.shape),
            fixed(head_gain.shape), rows_spec(2 * HEAD), rows_spec(2 * HEAD),
            fixed(cosine.shape), fixed(sine.shape),
        ],
        out_specs=[
            fixed(load), fixed(load), fixed((1, QK)), fixed((1, WIDTH)),
        ]
        + [fixed((rows, WIDTH)) for rows in PIECES],
        out_shape=[
            jax.ShapeDtypeStruct(load, BF16),
            jax.ShapeDtypeStruct(load, BF16),
            jax.ShapeDtypeStruct((1, QK), F32),
            jax.ShapeDtypeStruct((1, WIDTH), F32),
        ]
        + [jax.ShapeDtypeStruct((rows, WIDTH), BF16) for rows in PIECES],
        scratch_shapes=[
            pltpu.VMEM((TOKENS, WIDTH), BF16),
            pltpu.VMEM((K_HEADS, 2 * HEAD, GROUP), BF16),
            pltpu.VMEM((K_HEADS, GROUP, 2 * HEAD), F32),
            pltpu.VMEM((K_HEADS, GROUP, 2 * HEAD), F32),
            pltpu.VMEM((Q_LANES, WIDTH), F32),
            pltpu.VMEM((GROUP, QKV), BF16),
            pltpu.VMEM((2, *load), BF16),
        ],
        compiler_params=params(),
        cost_estimate=cost(Q_HEADS * GROUP * GROUP * 2 * 1280, 8 * MIB),
        name="attend_back",
    )(
        core, *grads, normed, normed_t, gain1, w_qkv, w_out, queries, keys, values, mixed, raw_q, raw_k, head_gain,
        cosine, sine, cosine, sine,
    )


def widen_kernel(core_ref, kept_ref, given_ref, q_ref, k_ref, v_ref, out_ref):
    rows = WIDTH // 2
    for half_ref, half in ((kept_ref, core_ref[0]), (given_ref, 1 - core_ref[0])):
        span = pl.ds(pl.multiple_of(half * rows, rows), rows)
        d_w = half_ref[:, :ROWS_QKV].astype(F32).reshape(rows, QKV)
        q_ref[span, :] = d_w[:, :Q_LANES]
        k_ref[span, :] = d_w[:, Q_LANES:QK]
        v_ref[span, :] = d_w[:, QK:]
        d_out = half_ref[:, ROWS_QKV : ROWS_QKV + 2 * ROWS_OUT].astype(F32)
        span = pl.ds(pl.multiple_of(half * (Q_LANES // 2), Q_LANES // 2), Q_LANES // 2)
        out_ref[span, :QKV] = d_out[:, :ROWS_OUT].reshape(Q_LANES // 2, QKV)
        out_ref[span, QKV:] = d_out[:, ROWS_OUT:].reshape(Q_LANES // 2, QKV)


def widen(core, kept, given):
    shapes = [(WIDTH, Q_LANES), (WIDTH, K_LANES), (WIDTH, K_LANES), (Q_LANES, WIDTH)]
    return pl.pallas_call(
        widen_kernel,
        grid=(1,),
        in_specs=[
            pl.BlockSpec(memory_space=pltpu.SMEM),
            fixed(kept.shape),
            fixed(given.shape),
        ],
        out_specs=[fixed(shape) for shape in shapes],
        out_shape=[jax.ShapeDtypeStruct(shape, F32) for shape in shapes],
        compiler_params=params(),
        cost_estimate=cost(0, 4 * MIB),
        name="widen",
    )(core, kept, given)


def turn_kernel(own_ref, lt_ref, lb_ref, rt_ref, rb_ref, *out_refs):
    rows = joined_sum(own_ref, (lt_ref, lb_ref), (rt_ref, rb_ref))
    for which, out_ref in enumerate(out_refs):
        out_ref[0] = rows[which * PIECE : (which + 1) * PIECE].T


def turn_over(pieces):
    out = jax.ShapeDtypeStruct((1, WIDTH, PIECE), F32)
    return pl.pallas_call(
        turn_kernel,
        grid=(1,),
        in_specs=[fixed(piece.shape) for piece in pieces],
        out_specs=[fixed(out.shape)] * 3,
        out_shape=[out] * 3,
        compiler_params=params(),
        cost_estimate=cost(0, 3 * MIB),
        name="turn",
    )(*pieces)


def norm1_kernel(hidden_ref, gain_ref, d_res_ref, own_ref, lt_ref, lb_ref, rt_ref, rb_ref, out_ref):
    d_normed = joined_sum(own_ref, (lt_ref, lb_ref), (rt_ref, rb_ref))
    back, _ = norm_back(hidden_ref[...].astype(F32), gain_ref[...], d_normed)
    out_ref[...] = d_res_ref[...] + back


def norm1_back(hidden, gain, d_residual, pieces):
    arrays = (hidden, gain, d_residual, *pieces)
    return pl.pallas_call(
        norm1_kernel,
        grid=(1,),
        in_specs=[fixed(array.shape) for array in arrays],
        out_specs=fixed(d_residual.shape),
        out_shape=jax.ShapeDtypeStruct(d_residual.shape, F32),
        compiler_params=params(),
        cost_estimate=cost(0, 4 * MIB),
        name="norm1_back",
    )(*arrays)


def store_halves(place, rows, out_refs):
    if place == 0:
        out_refs[0][...] = rows
    else:
        half = rows.shape[0] // 2
        out_refs[2 * place - 1][...] = rows[:half]
        out_refs[2 * place][...] = rows[half:]


def expert_kernel(first, last, slots, mine_ref, x_ref, c_ref, w_ref, wr_ref, *refs):
    if not first:
        (in_w_ref, in_r_ref, rank_ref, before_ref), refs = refs[:4], refs[4:]
    y_ref, dx_ref, out_r_ref, *refs = refs
    out_refs, (gate_ref, up_ref, down_ref, acc_ref, acc_r_ref) = refs[:-5], refs[-5:]
    step = pl.program_id(0)

    @pl.when(step == 0)
    def _():
        for shard in range(SHARDS):
            span = slice(shard * PIECE, (shard + 1) * PIECE)
            gate_ref[:, span] = w_ref[shard, 0]
            up_ref[:, span] = w_ref[shard, 1]
            down_ref[:, span] = w_ref[shard, 2]
        if first:
            acc_ref[...] = jnp.zeros_like(acc_ref)
            acc_r_ref[...] = jnp.zeros_like(acc_r_ref)
        else:
            acc_ref[...] = in_w_ref[...]
            acc_r_ref[...] = in_r_ref[...]

    count = SOURCES * slots
    rows = x_ref[...].reshape(count, WIDTH)
    cots = c_ref[...].reshape(count, WIDTH).astype(F32)
    logits = dot(rows, wr_ref[...])
    raised = jnp.exp(logits - jnp.max(logits, axis=-1, keepdims=True))
    router = raised / jnp.sum(raised, axis=-1, keepdims=True)
    own = lax.broadcasted_iota(jnp.int32, router.shape, 1) == mine_ref[0]
    gate = jnp.sum(jnp.where(own, router, 0.0), axis=-1, keepdims=True)
    gate_part = dot(rows, gate_ref[...])
    up_part = dot(rows, up_ref[...])
    s = 1.0 / (1.0 + jnp.exp(-gate_part))
    silu = gate_part * s
    inner = (silu * up_part).astype(BF16)
    result = dot_nt(inner, down_ref[...]).astype(BF16).astype(F32)
    weighted = (gate * result).astype(BF16).reshape(SOURCES, slots, WIDTH)
    if last:
        for source in range(SOURCES):
            pick = picks(rank_ref[source : source + 1, :], 0, CAP)
            slotted = jnp.concatenate([before_ref[source], weighted[source]], axis=0)
            y_ref[source] = dot_tn(pick, slotted).astype(BF16)
    else:
        y_ref[...] = weighted
    d_gate = jnp.sum(result * cots, axis=-1, keepdims=True)
    d_logits = (d_gate * router * (jnp.where(own, 1.0, 0.0) - gate)).astype(BF16)
    d_expert = (gate * cots).astype(BF16)
    d_inner = dot(d_expert, down_ref[...])
    d_g = (d_inner * up_part * s * (1.0 + gate_part * (1.0 - s))).astype(BF16)
    d_u = (d_inner * silu).astype(BF16)
    d_rows = dot_nt(d_g, gate_ref[...]) + dot_nt(d_u, up_ref[...]) + dot_nt(d_logits, wr_ref[...])
    dx_ref[...] = d_rows.astype(BF16).reshape(dx_ref.shape)
    acc_ref[0] += dot_tn(d_g, rows)
    acc_ref[1] += dot_tn(d_u, rows)
    acc_ref[2] += dot_tn(inner, d_expert)
    acc_r_ref[...] += dot_tn(d_logits, rows)

    @pl.when(step == EXPERTS // SOURCES - 1)
    def _():
        out_r_ref[...] = acc_r_ref[...]
        if last:
            for place in range(SHARDS):
                shard = (mine_ref[1] + place) % SHARDS
                span = pl.ds(pl.multiple_of(shard * PIECE, PIECE), PIECE)
                rows = jnp.concatenate([acc_ref[which, span, :] for which in range(3)], axis=0)
                store_halves(place, rows.astype(BF16), out_refs)
        else:
            out_refs[0][...] = acc_ref[...]


def expert(part, mine, rows, cots, weights, w_router, carried):
    first, last, slots = part == 0, part == len(PARTS) - 1, PARTS[part]
    assert sum(PARTS[:part]) % slots == 0
    place = sum(PARTS[:part]) // slots
    block = (SOURCES, slots, WIDTH)
    y_rows = TOKENS if last else slots
    out_w = [jax.ShapeDtypeStruct((3, FF, WIDTH), F32)]
    if last:
        whole, half = (3 * PIECE, WIDTH), (3 * PIECE // 2, WIDTH)
        out_w = [jax.ShapeDtypeStruct(whole, BF16)] + [jax.ShapeDtypeStruct(half, BF16)] * 6
    return pl.pallas_call(
        functools.partial(expert_kernel, first, last, slots),
        grid=(EXPERTS // SOURCES,),
        in_specs=[
            pl.BlockSpec(memory_space=pltpu.SMEM),
            pl.BlockSpec(block, lambda i: (i, 0, 0)),
            pl.BlockSpec(block, lambda i: (i, place, 0)),
            fixed(weights.shape),
            fixed(w_router.shape),
        ]
        + [fixed(array.shape) for array in carried[:2]]
        + [pl.BlockSpec((SOURCES, TOKENS), lambda i: (i, 0)) for _ in carried[2:3]]
        + [pl.BlockSpec(block, lambda i: (i, 0, 0)) for _ in carried[3:]],
        out_specs=[
            pl.BlockSpec((SOURCES, y_rows, WIDTH), lambda i: (i, 0, 0)),
            pl.BlockSpec(block, lambda i: (i, 0, 0)),
            fixed((EXPERTS, WIDTH)),
        ]
        + [fixed(out.shape) for out in out_w],
        out_shape=[
            jax.ShapeDtypeStruct((EXPERTS, y_rows, WIDTH), BF16),
            jax.ShapeDtypeStruct((EXPERTS, slots, WIDTH), BF16),
            jax.ShapeDtypeStruct((EXPERTS, WIDTH), F32),
        ]
        + out_w,
        scratch_shapes=[
            pltpu.VMEM((WIDTH, FF), BF16),
            pltpu.VMEM((WIDTH, FF), BF16),
            pltpu.VMEM((WIDTH, FF), BF16),
            pltpu.VMEM((3, FF, WIDTH), F32),
            pltpu.VMEM((EXPERTS, WIDTH), F32),
        ],
        compiler_params=params(E_MIB),
        cost_estimate=cost(18 * EXPERTS * slots * WIDTH * FF, 8 * EXPERTS * slots * WIDTH),
        name="expert",
    )(mine, rows, cots, weights, w_router, *carried)


def exchange(rows):
    return lax.all_to_all(rows, "expert", split_axis=0, concat_axis=0, tiled=True)


RING = ([(0, 1), (1, 2), (2, 3), (3, 0)], [(1, 0), (2, 1), (3, 2), (0, 3)])


def to_right(rows):
    return lax.ppermute(rows, "shard", RING[0])


def to_left(rows):
    return lax.ppermute(rows, "shard", RING[1])


def ring_gather(top, bottom):
    left_top, right_bottom = to_right(top), to_left(bottom)
    left_bottom, right_top = to_right(bottom), to_left(top)
    far_top, far_bottom = to_right(left_top), to_left(right_bottom)
    return (top, bottom, right_top, right_bottom, far_top, far_bottom, left_top, left_bottom)


def ring_scatter(own, right_top, right_bottom, far_top, far_bottom, left_top, left_bottom):
    to_add_top, to_add_bottom = to_right(far_top), to_left(far_bottom)
    from_left_bottom, from_right_top = to_right(right_bottom), to_left(left_top)
    from_left_top = to_right(added(right_top, to_add_top))
    from_right_bottom = to_left(added(left_bottom, to_add_bottom))
    return (own, from_left_top, from_left_bottom, from_right_top, from_right_bottom)


def added(one, other):
    return (one.astype(F32) + other.astype(F32)).astype(BF16)


SAME_CORE = [[2 * chip + core for chip in range(CHIPS)] for core in range(2)]


def exchange_same_core(rows):
    return lax.all_to_all(
        rows, "expert", split_axis=0, concat_axis=0, tiled=True, axis_index_groups=SAME_CORE
    )


def partner_rows(values, axis, size, bit):
    return lax.ppermute(values, axis, [(index, index ^ bit) for index in range(size)])


def swap_cores(rows):
    return partner_rows(rows, "expert", EXPERTS, 1)


def over_column(values):
    values = values + swap_cores(values)
    for bit in (1, 2):
        values = values + partner_rows(values, "shard", SHARDS, bit)
    return values


LATE = 3
SMALL = EXPERTS + LATE
SMALL_ROWS = -(-SMALL * (WIDTH // CHIPS) // QKV)
LOAD_ROWS = 64


def by_chip(small):
    return jnp.swapaxes(small.reshape(small.shape[0], CHIPS, -1), 0, 1).reshape(CHIPS, -1)


def pack_kernel(kept_ref, given_ref, small_ref, out_ref):
    first = ROWS_QKV + 2 * ROWS_OUT
    kept = kept_ref[...].astype(F32) + given_ref[...].astype(F32)
    out_ref[:, :first] = kept.astype(BF16)
    out_ref[:, first:] = three_pieces(small_ref[...], 1).astype(BF16)


def three_pieces(small, axis):
    high = small.astype(BF16).astype(F32)
    middle = (small - high).astype(BF16).astype(F32)
    low = small - high - middle
    rest = LOAD_ROWS - ROWS_QKV - 2 * ROWS_OUT - 3 * SMALL_ROWS
    blank = jnp.zeros_like(lax.slice_in_dim(small, 0, rest, axis=axis))
    return jnp.concatenate([high, middle, low, blank], axis=axis)


def pack(kept, given, small):
    out = jax.ShapeDtypeStruct((CHIPS, LOAD_ROWS, QKV), BF16)
    return pl.pallas_call(
        pack_kernel,
        grid=(1,),
        in_specs=[fixed(kept.shape), fixed(given.shape), fixed(small.shape)],
        out_specs=fixed(out.shape),
        out_shape=out,
        compiler_params=params(),
        cost_estimate=cost(0, 4 * MIB),
        name="pack",
    )(kept, given, small)


def add_kernel(pieces_ref, out_ref):
    first = ROWS_QKV + 2 * ROWS_OUT
    total = jnp.sum(pieces_ref[...].astype(F32), axis=0)
    small = total[first:]
    small = (
        small[:SMALL_ROWS] + small[SMALL_ROWS : 2 * SMALL_ROWS]
    ) + small[2 * SMALL_ROWS : 3 * SMALL_ROWS]
    rows = jnp.concatenate([total[:first], three_pieces(small, 0)], axis=0).astype(BF16)
    out_ref[...] = jnp.broadcast_to(rows[None], out_ref.shape)


def add_up(pieces):
    return pl.pallas_call(
        add_kernel,
        grid=(1,),
        in_specs=[fixed(pieces.shape)],
        out_specs=fixed(pieces.shape),
        out_shape=jax.ShapeDtypeStruct(pieces.shape, BF16),
        compiler_params=params(),
        cost_estimate=cost(0, 2 * MIB),
        name="add_up",
    )(pieces)


def after(value, *others):
    return lax.optimization_barrier((value, *others))[0]


def body(
    hidden_in, seq_lengths, routes, norm_gain1, w_query, w_key, w_value, query_gain, key_gain,
    w_out, norm_gain2, w_router, w_gate, w_up, w_down, cotangent,
):
    weights = jnp.stack([w_gate[0], w_up[0], w_down[0]], axis=0)
    routes_low = jnp.pad(routes.T.astype(BF16), ((0, 0), (0, WIDTH - TOKENS)))
    cots = lax.all_gather(jnp.concatenate([cotangent, routes_low], axis=0), "expert", axis=0)
    hidden_all = ring_gather(hidden_in[:HALF_ROWS], hidden_in[HALF_ROWS:])
    pick_first, place_first, pick_last, place_last = slot_tables(routes.T)

    lengths = seq_lengths[0]
    ends = jnp.cumsum(lengths)
    turn = lax.axis_index("shard").astype(jnp.int32) * TOKENS
    row_index = (jnp.arange(GROUP, dtype=jnp.int32) + turn) % GROUP
    segment = jnp.sum((row_index[:, None] >= ends[None, :]).astype(jnp.int32), axis=1)
    member = segment[:, None] == jnp.arange(lengths.shape[0], dtype=jnp.int32)[None, :]
    position = row_index - jnp.sum(jnp.where(member, (ends - lengths)[None, :], 0), axis=1)
    frequency = ROPE_BASE ** (-2.0 * jnp.arange(HALF, dtype=F32) / HEAD)
    angles = position.astype(F32)[:, None] * frequency[None, :]
    cosine, sine = jnp.cos(angles), jnp.sin(angles)
    cosine = jnp.concatenate([cosine] * 4, axis=1)
    sine = jnp.concatenate([-sine, sine] * 2, axis=1)
    feature_q = jnp.pad(member.astype(BF16), ((0, 0), (0, HEAD - 4)))
    feature_k = jnp.concatenate(
        [
            jnp.where(member, 0.0, -APART).astype(BF16),
            jnp.ones((GROUP, 3), BF16),
            jnp.zeros((GROUP, HEAD - 7), BF16),
        ],
        axis=1,
    )
    head_gain = jnp.concatenate([query_gain] * Q_HEADS + [key_gain] * K_HEADS)[None, :]
    gain1, gain2 = norm_gain1[None, :], norm_gain2[None, :]
    normed, raw_q, raw_k, keys, values, mixed, queries, *attended = attention(
        hidden_all, gain1, (w_query, w_key, w_value), head_gain, w_out, cosine, sine, feature_q, feature_k
    )
    attended = ring_scatter(*attended)
    weights = lax.all_gather(after(weights, *attended), "shard", axis=0)
    residual, rows, outgoing = norm2_dispatch(hidden_in, attended, gain2, pick_first)
    mine = jnp.stack([lax.axis_index("expert"), lax.axis_index("shard")]).astype(jnp.int32)
    arrived = [exchange(outgoing)]
    rows = after(rows, outgoing)
    cots, rank = collect(mine, after(cots, outgoing))
    normed_t = after(normed, outgoing).T
    w_qkv = jnp.concatenate(after((w_query, w_key, w_value), outgoing), axis=1)
    latest = exchange(after(dispatch(rows, pick_last), arrived[0], cots, normed_t))
    arrived.append(latest)
    carried, d_home = (), []
    for part, rows in enumerate(arrived):
        results, d_rows, d_r, *d_w = expert(part, mine, rows, cots, weights, w_router, carried)
        carried = (d_w[0], d_r, rank, results)
        latest = exchange(after(d_rows, latest))
        d_home.append(latest)
    d_router = d_r
    outputs = lax.psum_scatter(
        after(results, d_home[0]), "expert", scatter_dimension=0, tiled=False
    )

    d_experts = ring_scatter(*after(tuple(d_w), d_home[0]))
    d_router = over_column(after(d_router, d_home[0]))
    d_residual, d_top, d_bottom, gain2_share = norm2_back(
        residual, after(gain2, d_router, *d_experts), cotangent, (place_first, place_last), d_home
    )
    grads_all = ring_gather(d_top, d_bottom)
    core = mine[:1] % 2
    kept, given, head_share, gain1_share, *d_normed = attend_back(
        core, grads_all, normed, normed_t, gain1, w_qkv, w_out, queries, keys, values, mixed, raw_q, raw_k,
        head_gain, cosine, sine,
    )
    d_normed = ring_scatter(*d_normed)

    late = jnp.concatenate(
        [gain2_share, gain1_share, jnp.pad(head_share, ((0, 5), (0, WIDTH - QK)))], axis=0
    )
    small = jnp.concatenate([by_chip(d_router), by_chip(late[:LATE])], axis=1)
    small = jnp.pad(small, ((0, 0), (0, SMALL_ROWS * QKV - small.shape[1])))
    load = pack(kept, swap_cores(given), small.reshape(CHIPS, SMALL_ROWS, QKV))
    pieces = exchange_same_core(load)
    pieces, *d_normed = lax.optimization_barrier((pieces, *d_normed))
    whole = exchange_same_core(add_up(pieces))
    grad_hidden = norm1_back(hidden_in, gain1, d_residual, d_normed)
    hidden_out = (residual + outputs.astype(F32)).astype(BF16)

    d_experts = turn_over(d_experts)
    whole = after(whole, hidden_out, grad_hidden, d_experts[0])
    grad_w_q, grad_w_k, grad_w_v, grad_w_out = widen(core, whole, swap_cores(whole))
    first = ROWS_QKV + 2 * ROWS_OUT
    small = whole[:, first : first + 3 * SMALL_ROWS].astype(F32)
    small = jnp.sum(small.reshape(CHIPS, 3, -1), axis=1)[:, : SMALL * (WIDTH // CHIPS)]
    small = jnp.swapaxes(small.reshape(CHIPS, SMALL, -1), 0, 1).reshape(SMALL, WIDTH)
    late = over_column(small[EXPERTS:])
    head_share = late[2]
    return (
        hidden_out,
        grad_hidden,
        late[1],
        grad_w_q,
        grad_w_k,
        grad_w_v,
        jnp.sum(head_share[:Q_LANES].reshape(Q_HEADS, HEAD), axis=0),
        jnp.sum(head_share[Q_LANES:QK].reshape(K_HEADS, HEAD), axis=0),
        grad_w_out,
        late[0],
        small[:EXPERTS].T,
        *d_experts,
    )


def solution(mesh):
    in_specs = (
        P(("expert", "shard"), None),
        P("expert", None),
        P(("expert", "shard"), None),
        P(),
        P(None, "shard"),
        P(None, "shard"),
        P(None, "shard"),
        P(),
        P(),
        P("shard", None),
        P(),
        P(),
        P("expert", None, "shard"),
        P("expert", None, "shard"),
        P("expert", None, "shard"),
        P(("expert", "shard"), None),
    )
    out_specs = (
        P(("expert", "shard"), None),
        P(("expert", "shard"), None),
        P(),
        P(None, "shard"),
        P(None, "shard"),
        P(None, "shard"),
        P(),
        P(),
        P("shard", None),
        P(),
        P(),
        P("expert", None, "shard"),
        P("expert", None, "shard"),
        P("expert", None, "shard"),
    )
    return jax.shard_map(body, mesh=mesh, in_specs=in_specs, out_specs=out_specs, check_vma=False)
```

```python
import functools

import jax
import jax.numpy as jnp
from jax import lax
from jax.experimental import pallas as pl
from jax.experimental.pallas import tpu as pltpu
from jax.sharding import PartitionSpec as P

EXPERTS = 32
TOP = 8
CAP = 96
HEAD = 64
HALF = HEAD // 2
SHARDS = 4
GROUP = 1024
WIDTH = 1024
FF = 512

EPS_NORM = 1e-05
EPS_HEAD = 1e-06
ROPE_BASE = 10000.0
APART = 1024.0
MIB = 1 << 20
PIECE = FF // SHARDS

F32 = jnp.float32
BF16 = jnp.bfloat16
EXACT = lax.Precision.HIGHEST


def dot(left, right):
    return jnp.dot(left, right, preferred_element_type=F32)


def dot_nt(left, right):
    return lax.dot_general(left, right, (((1,), (1,)), ((), ())), preferred_element_type=F32)


def dot_tn(left, right):
    return lax.dot_general(left, right, (((0,), (0,)), ((), ())), preferred_element_type=F32)


def fixed(shape):
    zeros = (0,) * len(shape)
    return pl.BlockSpec(shape, lambda *_: zeros, pipeline_mode=pl.Buffered(1))


def params(mebibytes=60):
    return pltpu.CompilerParams(
        dimension_semantics=("arbitrary",), vmem_limit_bytes=mebibytes * MIB
    )


def cost(flops, moved):
    return pl.CostEstimate(flops=int(flops), bytes_accessed=int(moved), transcendentals=0)


def earlier_rows(named):
    tokens = named.shape[1]
    earlier = lax.broadcasted_iota(jnp.int32, (tokens, tokens), 0)
    later = lax.broadcasted_iota(jnp.int32, (tokens, tokens), 1)
    return dot(named.astype(BF16), jnp.where(earlier < later, 1.0, 0.0).astype(BF16))


def rank_table(routes_t):
    tokens = routes_t.shape[1]
    expert = lax.broadcasted_iota(jnp.int32, (EXPERTS, tokens), 0)
    named = jnp.zeros((EXPERTS, tokens), F32)
    for choice in range(TOP):
        named = named + jnp.where(routes_t[choice : choice + 1, :] == expert, 1.0, 0.0)
    return jnp.where(named > 0.5, earlier_rows(named), -1.0).astype(jnp.int32)


def picks(rank, first, slots):
    experts, tokens = rank.shape
    place = lax.broadcasted_iota(jnp.int32, (experts, slots, tokens), 1) + first
    hit = jnp.where(place == rank[:, None, :], 1.0, 0.0).astype(BF16)
    return hit.reshape(experts * slots, tokens)


TOKENS = GROUP // SHARDS
HALF_ROWS = TOKENS // 2
STEP_EXPERTS = 8
STEPS = EXPERTS // STEP_EXPERTS


SOURCES = 8
E_MIB = 60
ROUTE_LANES = TOKENS


def collect_kernel(mine_ref, all_ref, out_ref, rank_ref):
    named = []
    for source in range(SOURCES):
        routes = all_ref[source, TOKENS : TOKENS + TOP, :ROUTE_LANES].astype(F32)
        hits = jnp.where(routes == mine_ref[0].astype(F32), 1.0, 0.0)
        named.append(jnp.sum(hits, axis=0, keepdims=True))
    named = jnp.concatenate(named, axis=0)
    rank = jnp.where(named > 0.5, earlier_rows(named), -1.0).astype(jnp.int32)
    rank_ref[...] = rank
    for source in range(SOURCES):
        pick = picks(rank[source : source + 1, :], 0, CAP)
        out_ref[source] = dot(pick, all_ref[source, :TOKENS, :]).astype(BF16)


def collect(mine, gathered):
    rows = gathered.shape[1]
    return pl.pallas_call(
        collect_kernel,
        grid=(EXPERTS // SOURCES,),
        in_specs=[
            pl.BlockSpec(memory_space=pltpu.SMEM),
            pl.BlockSpec((SOURCES, rows, WIDTH), lambda i: (i, 0, 0)),
        ],
        out_specs=[
            pl.BlockSpec((SOURCES, CAP, WIDTH), lambda i: (i, 0, 0)),
            pl.BlockSpec((SOURCES, TOKENS), lambda i: (i, 0)),
        ],
        out_shape=[
            jax.ShapeDtypeStruct((EXPERTS, CAP, WIDTH), BF16),
            jax.ShapeDtypeStruct((EXPERTS, TOKENS), jnp.int32),
        ],
        compiler_params=params(),
        cost_estimate=cost(2 * EXPERTS * CAP * TOKENS * WIDTH, 24 * MIB),
        name="collect",
    )(mine, gathered)


PARTS = (48, 48)


def slots_kernel(routes_ref, *refs):
    rank = rank_table(routes_ref[...])
    first = 0
    for part, slots in enumerate(PARTS):
        pick = picks(rank, first, slots)
        refs[2 * part][...] = pick
        refs[2 * part + 1][...] = pick.T
        first += slots


def slot_tables(routes_t):
    shapes = []
    for slots in PARTS:
        shapes += [(EXPERTS * slots, TOKENS), (TOKENS, EXPERTS * slots)]
    return pl.pallas_call(
        slots_kernel,
        grid=(1,),
        in_specs=[fixed(routes_t.shape)],
        out_specs=[fixed(shape) for shape in shapes],
        out_shape=[jax.ShapeDtypeStruct(shape, BF16) for shape in shapes],
        compiler_params=params(),
        cost_estimate=cost(0, 4 * MIB),
        name="slot_tables",
    )(routes_t)


def joined_sum(own_ref, from_left, from_right):
    halves = []
    rows = own_ref.shape[0] // 2
    for half in range(2):
        span = slice(half * rows, (half + 1) * rows)
        halves.append(
            own_ref[span, :].astype(F32)
            + from_left[half][...].astype(F32)
            + from_right[half][...].astype(F32)
        )
    return jnp.concatenate(halves, axis=0)


def norm2_kernel(hidden_ref, own_ref, lt_ref, lb_ref, rt_ref, rb_ref, gain_ref, *refs):
    pick_ref, res_ref, rows_ref, out_ref = refs

    @pl.when(pl.program_id(0) == 0)
    def _():
        attended = joined_sum(own_ref, (lt_ref, lb_ref), (rt_ref, rb_ref))
        residual = hidden_ref[...].astype(F32) + attended
        res_ref[...] = residual
        scale = lax.rsqrt(jnp.mean(residual * residual, axis=-1, keepdims=True) + EPS_NORM)
        rows_ref[...] = (residual * scale * gain_ref[...]).astype(BF16)

    out_ref[...] = dot(pick_ref[...], rows_ref[...]).astype(BF16).reshape(out_ref.shape)


def dispatch_kernel(pick_ref, rows_ref, out_ref):
    out_ref[...] = dot(pick_ref[...], rows_ref[...]).astype(BF16).reshape(out_ref.shape)


def dispatch(rows, pick):
    slots = pick.shape[0] // EXPERTS
    tokens = rows.shape[0]
    return pl.pallas_call(
        dispatch_kernel,
        grid=(STEPS,),
        in_specs=[
            pl.BlockSpec((STEP_EXPERTS * slots, tokens), lambda i: (i, 0)),
            fixed(rows.shape),
        ],
        out_specs=pl.BlockSpec((STEP_EXPERTS, slots, WIDTH), lambda i: (i, 0, 0)),
        out_shape=jax.ShapeDtypeStruct((EXPERTS, slots, WIDTH), BF16),
        compiler_params=params(),
        cost_estimate=cost(2 * EXPERTS * slots * tokens * WIDTH, 2 * EXPERTS * slots * WIDTH),
        name="dispatch",
    )(pick, rows)


def norm2_dispatch(hidden, attended, gain, pick):
    whole = (hidden, *attended, gain)
    tokens = hidden.shape[0]
    slots = pick.shape[0] // EXPERTS
    return pl.pallas_call(
        norm2_kernel,
        grid=(STEPS,),
        in_specs=[fixed(array.shape) for array in whole]
        + [pl.BlockSpec((STEP_EXPERTS * slots, tokens), lambda i: (i, 0))],
        out_specs=[
            fixed((tokens, WIDTH)),
            fixed((tokens, WIDTH)),
            pl.BlockSpec((STEP_EXPERTS, slots, WIDTH), lambda i: (i, 0, 0)),
        ],
        out_shape=[
            jax.ShapeDtypeStruct((tokens, WIDTH), F32),
            jax.ShapeDtypeStruct((tokens, WIDTH), BF16),
            jax.ShapeDtypeStruct((EXPERTS, slots, WIDTH), BF16),
        ],
        compiler_params=params(),
        cost_estimate=cost(2 * EXPERTS * slots * tokens * WIDTH, 2 * EXPERTS * slots * WIDTH),
        name="norm2_dispatch",
    )(*whole, pick)


def norm_back(rows, gain, grad):
    scale = lax.rsqrt(jnp.mean(rows * rows, axis=-1, keepdims=True) + EPS_NORM)
    scaled = grad * gain
    inner = jnp.mean(scaled * rows, axis=-1, keepdims=True)
    return scale * scaled - rows * (scale * scale * scale * inner), grad * rows * scale


def norm2_back_kernel(res_ref, gain_ref, cot_ref, *refs):
    place_refs, part_refs = refs[: len(PARTS)], refs[len(PARTS) : 2 * len(PARTS)]
    grad_ref, top_ref, bottom_ref, share_ref, total_ref = refs[2 * len(PARTS) :]
    step = pl.program_id(0)
    total = jnp.zeros(total_ref.shape, F32)
    for place_ref, part_ref, slots in zip(place_refs, part_refs, PARTS):
        total += dot(place_ref[...], part_ref[...].reshape(STEP_EXPERTS * slots, WIDTH))

    @pl.when(step == 0)
    def _():
        total_ref[...] = total

    @pl.when(step > 0)
    def _():
        total_ref[...] += total

    @pl.when(step == STEPS - 1)
    def _():
        back, share = norm_back(res_ref[...], gain_ref[...], total_ref[...])
        grad = cot_ref[...].astype(F32) + back
        grad_ref[...] = grad
        top_ref[...] = grad[:HALF_ROWS].astype(BF16)
        bottom_ref[...] = grad[HALF_ROWS:].astype(BF16)
        share_ref[...] = jnp.sum(share, axis=0, keepdims=True)


def norm2_back(residual, gain, cotangent, places, parts):
    whole = (residual, gain, cotangent)
    tokens = residual.shape[0]
    return pl.pallas_call(
        norm2_back_kernel,
        grid=(STEPS,),
        in_specs=[fixed(array.shape) for array in whole]
        + [pl.BlockSpec((tokens, STEP_EXPERTS * slots), lambda i: (0, i)) for slots in PARTS]
        + [pl.BlockSpec((STEP_EXPERTS, slots, WIDTH), lambda i: (i, 0, 0)) for slots in PARTS],
        out_specs=[
            fixed((tokens, WIDTH)),
            fixed((HALF_ROWS, WIDTH)),
            fixed((HALF_ROWS, WIDTH)),
            fixed((1, WIDTH)),
        ],
        out_shape=[
            jax.ShapeDtypeStruct((tokens, WIDTH), F32),
            jax.ShapeDtypeStruct((HALF_ROWS, WIDTH), BF16),
            jax.ShapeDtypeStruct((HALF_ROWS, WIDTH), BF16),
            jax.ShapeDtypeStruct((1, WIDTH), F32),
        ],
        scratch_shapes=[pltpu.VMEM((tokens, WIDTH), F32)],
        compiler_params=params(24),
        cost_estimate=cost(2 * EXPERTS * CAP * tokens * WIDTH, 2 * EXPERTS * CAP * WIDTH),
        name="norm2_back",
    )(*whole, *places, *parts)


ROW_STEP = 256
ROW_STEPS = GROUP // ROW_STEP
Q_LANES = 256
K_LANES = 128
QK = Q_LANES + K_LANES
QKV = QK + K_LANES
CHIPS = EXPERTS // 2
ROWS_QKV = WIDTH // EXPERTS
ROWS_OUT = Q_LANES // EXPERTS
Q_HEADS = Q_LANES // HEAD
K_HEADS = K_LANES // HEAD
RATIO = Q_HEADS // K_HEADS
LSE_LANE = HEAD + 4


def head_mean(values):
    lanes = values.shape[1]
    row = lax.broadcasted_iota(jnp.int32, (lanes, lanes), 0) // HEAD
    column = lax.broadcasted_iota(jnp.int32, (lanes, lanes), 1) // HEAD
    share = jnp.where(row == column, 1.0 / HEAD, 0.0).astype(F32)
    return jnp.dot(values, share, preferred_element_type=F32, precision=EXACT)


def partner(values):
    lanes = values.shape[1]
    ahead = pltpu.roll(values, lanes - HALF, 1)
    behind = pltpu.roll(values, HALF, 1)
    lane = lax.broadcasted_iota(jnp.int32, values.shape, 1)
    return jnp.where(lane % HEAD < HALF, ahead, behind)


def choose(step, pieces, block_ref):
    for place in range(SHARDS):
        refs = pieces[2 * place : 2 * place + 2]

        @pl.when(step == place)
        def _(refs=refs):
            first = 0
            for ref in refs:
                block_ref[first : first + ref.shape[0], :] = ref[...]
                first += ref.shape[0]


def prep_block(rows, step, gain_ref, w_refs, head_gain_ref, cos_ref, sin_ref, fq_ref, fk_ref, refs):
    normed_ref, raw_q_ref, raw_k_ref, q_ref, k_ref, v_ref = refs
    hidden = rows.astype(F32)
    scale = lax.rsqrt(jnp.mean(hidden * hidden, axis=-1, keepdims=True) + EPS_NORM)
    normed = (hidden * scale * gain_ref[...]).astype(BF16)
    normed_ref[...] = normed
    all_three = jnp.concatenate([dot(normed, w_ref[...]) for w_ref in w_refs], axis=1)
    raw = all_three[:, :QK]
    raw_q_ref[...] = raw[:, :Q_LANES]
    raw_k_ref[...] = raw[:, Q_LANES:]
    scaled = raw * lax.rsqrt(head_mean(raw * raw) + EPS_HEAD) * head_gain_ref[...]
    cosine = jnp.concatenate([cos_ref[...]] * 3, axis=1)
    sine = jnp.concatenate([sin_ref[...]] * 3, axis=1)
    turned = scaled * cosine + partner(scaled) * sine
    span = pl.ds(pl.multiple_of(step * ROW_STEP, ROW_STEP), ROW_STEP)
    for head in range(Q_HEADS):
        part = turned[:, head * HEAD : (head + 1) * HEAD].astype(BF16)
        q_ref[head, span, :] = jnp.concatenate([part * BF16(HEAD**-0.5), fq_ref[...]], axis=1)
    for head in range(K_HEADS):
        first = Q_LANES + head * HEAD
        part = turned[:, first : first + HEAD].astype(BF16)
        k_ref[head, span, :] = jnp.concatenate([part, fk_ref[...]], axis=1)
        value = all_three[:, QK + head * HEAD : QK + (head + 1) * HEAD].astype(BF16)
        v_ref[head, span, :] = jnp.concatenate([value, jnp.ones_like(value)], axis=1)


def attention_kernel(
    h0_ref, h1_ref, h2_ref, h3_ref, h4_ref, h5_ref, h6_ref, h7_ref, gain_ref,
    wq_ref, wk_ref, wv_ref, head_gain_ref, w_out_ref, cos_ref, sin_ref, fq_ref, fk_ref,
    normed_ref, raw_q_ref, raw_k_ref, k_ref, v_ref, mixed_ref, q2_ref, *refs,
):
    out_refs, (block_ref, q_ref) = refs[:-2], refs[-2:]
    step = pl.program_id(0)

    @pl.when(step < ROW_STEPS)
    def _():
        pieces = (h0_ref, h1_ref, h2_ref, h3_ref, h4_ref, h5_ref, h6_ref, h7_ref)
        choose(step, pieces, block_ref)
        prep_block(
            block_ref[...], step, gain_ref, (wq_ref, wk_ref, wv_ref), head_gain_ref, cos_ref, sin_ref, fq_ref, fk_ref,
            (normed_ref, raw_q_ref, raw_k_ref, q_ref, k_ref, v_ref),
        )

    @pl.when(step >= ROW_STEPS)
    def _():
        attend_block(
            step - ROW_STEPS, q_ref, k_ref, v_ref, w_out_ref, mixed_ref, q2_ref, out_refs
        )


def rows_spec(lanes):
    return pl.BlockSpec((ROW_STEP, lanes), lambda i: (i, 0))


def heads_spec(heads):
    return pl.BlockSpec((heads, ROW_STEP, 2 * HEAD), lambda i: (0, i, 0))


PLACES = (
    ((0, TOKENS),),
    ((0, HALF_ROWS), (HALF_ROWS, TOKENS)),
    ((0, HALF_ROWS), (HALF_ROWS, TOKENS)),
    ((0, HALF_ROWS), (HALF_ROWS, TOKENS)),
)
PIECES = [last - first for place in PLACES for first, last in place]


def store_pieces(place, rows, out_refs):
    before = sum(len(spans) for spans in PLACES[:place])
    for ref, (first, last) in zip(out_refs[before:], PLACES[place]):
        ref[...] = rows[first:last]


def attend_block(step, q_ref, k_ref, v_ref, w_ref, mixed_ref, q2_ref, out_refs):
    span = pl.ds(pl.multiple_of(step * ROW_STEP, ROW_STEP), ROW_STEP)
    lane = lax.broadcasted_iota(jnp.int32, (RATIO * ROW_STEP, 2 * HEAD), 1)
    heads = []
    for group in range(K_HEADS):
        queries = q_ref[group * RATIO : (group + 1) * RATIO, span, :]
        queries = queries.reshape(RATIO * ROW_STEP, 2 * HEAD)
        scores = dot_nt(queries, k_ref[group])
        weights = jnp.exp(scores).astype(BF16)
        summed = dot(weights, v_ref[group])
        total = summed[:, HEAD : HEAD + 1]
        mixed = (summed[:, :HEAD] / total).astype(BF16)
        less = -jnp.log(total)
        high = less.astype(BF16).astype(F32)
        middle = (less - high).astype(BF16).astype(F32)
        low = less - high - middle
        extra = jnp.where(
            lane == LSE_LANE,
            high,
            jnp.where(lane == LSE_LANE + 1, middle, jnp.where(lane == LSE_LANE + 2, low, 0.0)),
        )
        q2_ref[group * RATIO : (group + 1) * RATIO] = (
            (queries.astype(F32) + extra).astype(BF16).reshape(RATIO, ROW_STEP, 2 * HEAD)
        )
        for head in range(RATIO):
            heads.append(mixed[head * ROW_STEP : (head + 1) * ROW_STEP])
    joined = jnp.concatenate(heads, axis=1)
    mixed_ref[...] = joined
    rows = dot(joined, w_ref[...]).astype(BF16)
    for place in range(SHARDS):

        @pl.when(step == place)
        def _(place=place):
            store_pieces(place, rows, out_refs)


def early_rows(lanes):
    return pl.BlockSpec((ROW_STEP, lanes), lambda i: (jnp.minimum(i, ROW_STEPS - 1), 0))


def late_rows(lanes):
    return pl.BlockSpec((ROW_STEP, lanes), lambda i: (jnp.maximum(i - ROW_STEPS, 0), 0))


def attention(hidden, gain, weights, head_gain, w_out, cosine, sine, feature_q, feature_k):
    whole = (*hidden, gain, *weights, head_gain, w_out)
    kept = (K_HEADS, GROUP, 2 * HEAD)
    return pl.pallas_call(
        attention_kernel,
        grid=(2 * ROW_STEPS,),
        in_specs=[fixed(array.shape) for array in whole]
        + [early_rows(2 * HEAD), early_rows(2 * HEAD), early_rows(HEAD), early_rows(HEAD)],
        out_specs=[
            early_rows(WIDTH), early_rows(Q_LANES), early_rows(K_LANES), fixed(kept), fixed(kept),
            late_rows(Q_LANES),
            pl.BlockSpec(
                (Q_HEADS, ROW_STEP, 2 * HEAD), lambda i: (0, jnp.maximum(i - ROW_STEPS, 0), 0)
            ),
        ]
        + [fixed((rows, WIDTH)) for rows in PIECES],
        out_shape=[
            jax.ShapeDtypeStruct((GROUP, WIDTH), BF16),
            jax.ShapeDtypeStruct((GROUP, Q_LANES), F32),
            jax.ShapeDtypeStruct((GROUP, K_LANES), F32),
            jax.ShapeDtypeStruct(kept, BF16),
            jax.ShapeDtypeStruct(kept, BF16),
            jax.ShapeDtypeStruct((GROUP, Q_LANES), BF16),
            jax.ShapeDtypeStruct((Q_HEADS, GROUP, 2 * HEAD), BF16),
        ]
        + [jax.ShapeDtypeStruct((rows, WIDTH), BF16) for rows in PIECES],
        scratch_shapes=[
            pltpu.VMEM((TOKENS, WIDTH), BF16),
            pltpu.VMEM((Q_HEADS, GROUP, 2 * HEAD), BF16),
        ],
        compiler_params=params(),
        cost_estimate=cost(Q_HEADS * GROUP * GROUP * 2 * 512 + 2 * GROUP * WIDTH * 512, 16 * MIB),
        name="attention",
    )(*whole, cosine, sine, feature_q, feature_k)


def turn_back(grad, raw, gain, cosine, sine):
    grad = grad * cosine - partner(grad) * sine
    scale = lax.rsqrt(head_mean(raw * raw) + EPS_HEAD)
    scaled = grad * gain
    inner = head_mean(scaled * raw)
    back = scale * scaled - raw * (scale * scale * scale * inner)
    return back, jnp.sum(grad * raw * scale, axis=0, keepdims=True)


def attend_back_kernel(
    core_ref, h0_ref, h1_ref, h2_ref, h3_ref, h4_ref, h5_ref, h6_ref, h7_ref,
    normed_ref, normed_t_ref, gain1_ref, w_qkv_ref, w_ref, q2_ref, k_ref, v_ref, mixed_ref, raw_q_ref, raw_k_ref, gain_ref,
    cos_ref, sin_ref, cos_k_ref, sin_k_ref,
    kept_ref, given_ref, share_ref, share1_ref, *refs,
):
    out_refs, refs = refs[:-7], refs[-7:]
    grad_ref, kt_ref, dk_ref, dv_ref, d_out_acc, d_qkv_ref, load_ref = refs
    step = pl.program_id(0)
    choose(step, (h0_ref, h1_ref, h2_ref, h3_ref, h4_ref, h5_ref, h6_ref, h7_ref), grad_ref)

    @pl.when(step == 0)
    def _():
        for group in range(K_HEADS):
            kt_ref[group] = k_ref[group].T
        dk_ref[...] = jnp.zeros_like(dk_ref)
        dv_ref[...] = jnp.zeros_like(dv_ref)
        share_ref[...] = jnp.zeros_like(share_ref)
        d_out_acc[...] = jnp.zeros_like(d_out_acc)

    d_out_acc[...] += dot_tn(mixed_ref[...], grad_ref[...])
    d_mixed = dot_nt(grad_ref[...], w_ref[...]).astype(BF16)
    wide = d_mixed.astype(F32)
    product = wide * mixed_ref[...].astype(F32)
    lane = lax.broadcasted_iota(jnp.int32, (ROW_STEP, HEAD), 1)
    heads = []
    for head in range(Q_HEADS):
        span = slice(head * HEAD, (head + 1) * HEAD)
        less = -jnp.sum(product[:, span], axis=1, keepdims=True)
        high = less.astype(BF16).astype(F32)
        middle = (less - high).astype(BF16).astype(F32)
        low = less - high - middle
        extra = jnp.where(
            lane == 0, high, jnp.where(lane == 1, middle, jnp.where(lane == 2, low, 0.0))
        )
        heads.append(jnp.concatenate([wide[:, span], extra], axis=1).astype(BF16))
    d_queries = []
    for group in range(K_HEADS):
        queries = q2_ref[group * RATIO : (group + 1) * RATIO].reshape(RATIO * ROW_STEP, 2 * HEAD)
        grads = jnp.concatenate(heads[group * RATIO : (group + 1) * RATIO], axis=0)
        probs = jnp.exp(dot_nt(k_ref[group], queries))
        d_scores = (probs * dot_nt(v_ref[group], grads)).astype(BF16)
        dv_ref[group] += dot(probs.astype(BF16), grads)
        dk_ref[group] += dot(d_scores, queries)
        turned = dot(kt_ref[group], d_scores)[:HEAD].T * (HEAD**-0.5)
        for head in range(RATIO):
            d_queries.append(turned[head * ROW_STEP : (head + 1) * ROW_STEP])
    cosine, sine = cos_ref[...], sin_ref[...]
    back, share = turn_back(
        jnp.concatenate(d_queries, axis=1),
        raw_q_ref[...],
        gain_ref[:, :Q_LANES],
        jnp.concatenate([cosine, cosine], axis=1),
        jnp.concatenate([sine, sine], axis=1),
    )
    d_qkv_ref[pl.ds(pl.multiple_of(step * ROW_STEP, ROW_STEP), ROW_STEP), :Q_LANES] = back.astype(BF16)
    share_ref[:, :Q_LANES] += share

    @pl.when(step == ROW_STEPS - 1)
    def _():
        d_keys = jnp.concatenate([dk_ref[group][:, :HEAD] for group in range(K_HEADS)], axis=1)
        back_k, share_k = turn_back(
            d_keys, raw_k_ref[...], gain_ref[:, Q_LANES:], cos_k_ref[...], sin_k_ref[...]
        )
        d_values = jnp.concatenate([dv_ref[group][:, :HEAD] for group in range(K_HEADS)], axis=1)
        d_qkv_ref[:, Q_LANES:] = jnp.concatenate([back_k, d_values], axis=1).astype(BF16)
        share_ref[:, Q_LANES:] = share_k
        d_w = dot(normed_t_ref[...], d_qkv_ref[...]).astype(BF16)
        load_ref[:, :, :ROWS_QKV] = d_w.reshape(2, CHIPS, ROWS_QKV, QKV)
        d_out = d_out_acc[...].reshape(EXPERTS, ROWS_OUT, WIDTH)
        d_out = jnp.concatenate([d_out[:, :, :QKV], d_out[:, :, QKV:]], axis=1).astype(BF16)
        load_ref[:, :, ROWS_QKV:] = d_out.reshape(2, CHIPS, 2 * ROWS_OUT, QKV)
        kept_ref[...] = load_ref[core_ref[0]]
        given_ref[...] = load_ref[1 - core_ref[0]]
        share1 = jnp.zeros((1, WIDTH), F32)
        for place in range(SHARDS):
            span = slice(place * TOKENS, (place + 1) * TOKENS)
            d_normed = dot_nt(d_qkv_ref[span, :], w_qkv_ref[...])
            store_pieces(place, d_normed.astype(BF16), out_refs)
            share1 += jnp.sum(d_normed * normed_ref[span, :].astype(F32), axis=0, keepdims=True)
        share1_ref[...] = share1 / gain1_ref[...]


def attend_back(
    core, grads, normed, normed_t, gain1, w_qkv, w_out, queries, keys, values, mixed, raw_q, raw_k, head_gain,
    cosine, sine,
):
    load = (CHIPS, ROWS_QKV + 2 * ROWS_OUT, QKV)
    return pl.pallas_call(
        attend_back_kernel,
        grid=(ROW_STEPS,),
        in_specs=[
            pl.BlockSpec(memory_space=pltpu.SMEM),
            *[fixed(piece.shape) for piece in grads],
            fixed(normed.shape), fixed(normed_t.shape), fixed(gain1.shape), fixed(w_qkv.shape),
            fixed(w_out.shape), heads_spec(Q_HEADS), fixed(keys.shape),
            fixed(values.shape), rows_spec(Q_LANES), rows_spec(Q_LANES), fixed(raw_k.shape),
            fixed(head_gain.shape), rows_spec(2 * HEAD), rows_spec(2 * HEAD),
            fixed(cosine.shape), fixed(sine.shape),
        ],
        out_specs=[
            fixed(load), fixed(load), fixed((1, QK)), fixed((1, WIDTH)),
        ]
        + [fixed((rows, WIDTH)) for rows in PIECES],
        out_shape=[
            jax.ShapeDtypeStruct(load, BF16),
            jax.ShapeDtypeStruct(load, BF16),
            jax.ShapeDtypeStruct((1, QK), F32),
            jax.ShapeDtypeStruct((1, WIDTH), F32),
        ]
        + [jax.ShapeDtypeStruct((rows, WIDTH), BF16) for rows in PIECES],
        scratch_shapes=[
            pltpu.VMEM((TOKENS, WIDTH), BF16),
            pltpu.VMEM((K_HEADS, 2 * HEAD, GROUP), BF16),
            pltpu.VMEM((K_HEADS, GROUP, 2 * HEAD), F32),
            pltpu.VMEM((K_HEADS, GROUP, 2 * HEAD), F32),
            pltpu.VMEM((Q_LANES, WIDTH), F32),
            pltpu.VMEM((GROUP, QKV), BF16),
            pltpu.VMEM((2, *load), BF16),
        ],
        compiler_params=params(),
        cost_estimate=cost(Q_HEADS * GROUP * GROUP * 2 * 1280, 8 * MIB),
        name="attend_back",
    )(
        core, *grads, normed, normed_t, gain1, w_qkv, w_out, queries, keys, values, mixed, raw_q, raw_k, head_gain,
        cosine, sine, cosine, sine,
    )


def widen_kernel(core_ref, kept_ref, given_ref, q_ref, k_ref, v_ref, out_ref):
    rows = WIDTH // 2
    for half_ref, half in ((kept_ref, core_ref[0]), (given_ref, 1 - core_ref[0])):
        span = pl.ds(pl.multiple_of(half * rows, rows), rows)
        d_w = half_ref[:, :ROWS_QKV].astype(F32).reshape(rows, QKV)
        q_ref[span, :] = d_w[:, :Q_LANES]
        k_ref[span, :] = d_w[:, Q_LANES:QK]
        v_ref[span, :] = d_w[:, QK:]
        d_out = half_ref[:, ROWS_QKV : ROWS_QKV + 2 * ROWS_OUT].astype(F32)
        span = pl.ds(pl.multiple_of(half * (Q_LANES // 2), Q_LANES // 2), Q_LANES // 2)
        out_ref[span, :QKV] = d_out[:, :ROWS_OUT].reshape(Q_LANES // 2, QKV)
        out_ref[span, QKV:] = d_out[:, ROWS_OUT:].reshape(Q_LANES // 2, QKV)


def widen(core, kept, given):
    shapes = [(WIDTH, Q_LANES), (WIDTH, K_LANES), (WIDTH, K_LANES), (Q_LANES, WIDTH)]
    return pl.pallas_call(
        widen_kernel,
        grid=(1,),
        in_specs=[
            pl.BlockSpec(memory_space=pltpu.SMEM),
            fixed(kept.shape),
            fixed(given.shape),
        ],
        out_specs=[fixed(shape) for shape in shapes],
        out_shape=[jax.ShapeDtypeStruct(shape, F32) for shape in shapes],
        compiler_params=params(),
        cost_estimate=cost(0, 4 * MIB),
        name="widen",
    )(core, kept, given)


def turn_kernel(own_ref, lt_ref, lb_ref, rt_ref, rb_ref, *out_refs):
    rows = joined_sum(own_ref, (lt_ref, lb_ref), (rt_ref, rb_ref))
    for which, out_ref in enumerate(out_refs):
        out_ref[0] = rows[which * PIECE : (which + 1) * PIECE].T


def turn_over(pieces):
    out = jax.ShapeDtypeStruct((1, WIDTH, PIECE), F32)
    return pl.pallas_call(
        turn_kernel,
        grid=(1,),
        in_specs=[fixed(piece.shape) for piece in pieces],
        out_specs=[fixed(out.shape)] * 3,
        out_shape=[out] * 3,
        compiler_params=params(),
        cost_estimate=cost(0, 3 * MIB),
        name="turn",
    )(*pieces)


def norm1_kernel(hidden_ref, gain_ref, d_res_ref, own_ref, lt_ref, lb_ref, rt_ref, rb_ref, out_ref):
    d_normed = joined_sum(own_ref, (lt_ref, lb_ref), (rt_ref, rb_ref))
    back, _ = norm_back(hidden_ref[...].astype(F32), gain_ref[...], d_normed)
    out_ref[...] = d_res_ref[...] + back


def norm1_back(hidden, gain, d_residual, pieces):
    arrays = (hidden, gain, d_residual, *pieces)
    return pl.pallas_call(
        norm1_kernel,
        grid=(1,),
        in_specs=[fixed(array.shape) for array in arrays],
        out_specs=fixed(d_residual.shape),
        out_shape=jax.ShapeDtypeStruct(d_residual.shape, F32),
        compiler_params=params(),
        cost_estimate=cost(0, 4 * MIB),
        name="norm1_back",
    )(*arrays)


def store_halves(place, rows, out_refs):
    if place == 0:
        out_refs[0][...] = rows
    else:
        half = rows.shape[0] // 2
        out_refs[2 * place - 1][...] = rows[:half]
        out_refs[2 * place][...] = rows[half:]


def expert_kernel(first, last, slots, mine_ref, x_ref, c_ref, w_ref, wr_ref, *refs):
    if not first:
        (in_w_ref, in_r_ref, rank_ref, before_ref), refs = refs[:4], refs[4:]
    y_ref, dx_ref, out_r_ref, *refs = refs
    out_refs, (gate_ref, up_ref, down_ref, acc_ref, acc_r_ref) = refs[:-5], refs[-5:]
    step = pl.program_id(0)

    @pl.when(step == 0)
    def _():
        for shard in range(SHARDS):
            span = slice(shard * PIECE, (shard + 1) * PIECE)
            gate_ref[:, span] = w_ref[shard, 0]
            up_ref[:, span] = w_ref[shard, 1]
            down_ref[:, span] = w_ref[shard, 2]
        if first:
            acc_ref[...] = jnp.zeros_like(acc_ref)
            acc_r_ref[...] = jnp.zeros_like(acc_r_ref)
        else:
            acc_ref[...] = in_w_ref[...]
            acc_r_ref[...] = in_r_ref[...]

    count = SOURCES * slots
    rows = x_ref[...].reshape(count, WIDTH)
    cots = c_ref[...].reshape(count, WIDTH).astype(F32)
    logits = dot(rows, wr_ref[...])
    raised = jnp.exp(logits - jnp.max(logits, axis=-1, keepdims=True))
    router = raised / jnp.sum(raised, axis=-1, keepdims=True)
    own = lax.broadcasted_iota(jnp.int32, router.shape, 1) == mine_ref[0]
    gate = jnp.sum(jnp.where(own, router, 0.0), axis=-1, keepdims=True)
    gate_part = dot(rows, gate_ref[...])
    up_part = dot(rows, up_ref[...])
    s = 1.0 / (1.0 + jnp.exp(-gate_part))
    silu = gate_part * s
    inner = (silu * up_part).astype(BF16)
    result = dot_nt(inner, down_ref[...]).astype(BF16).astype(F32)
    weighted = (gate * result).astype(BF16).reshape(SOURCES, slots, WIDTH)
    if last:
        for source in range(SOURCES):
            pick = picks(rank_ref[source : source + 1, :], 0, CAP)
            slotted = jnp.concatenate([before_ref[source], weighted[source]], axis=0)
            y_ref[source] = dot_tn(pick, slotted).astype(BF16)
    else:
        y_ref[...] = weighted
    d_gate = jnp.sum(result * cots, axis=-1, keepdims=True)
    d_logits = (d_gate * router * (jnp.where(own, 1.0, 0.0) - gate)).astype(BF16)
    d_expert = (gate * cots).astype(BF16)
    d_inner = dot(d_expert, down_ref[...])
    d_g = (d_inner * up_part * s * (1.0 + gate_part * (1.0 - s))).astype(BF16)
    d_u = (d_inner * silu).astype(BF16)
    d_rows = dot_nt(d_g, gate_ref[...]) + dot_nt(d_u, up_ref[...]) + dot_nt(d_logits, wr_ref[...])
    dx_ref[...] = d_rows.astype(BF16).reshape(dx_ref.shape)
    acc_ref[0] += dot_tn(d_g, rows)
    acc_ref[1] += dot_tn(d_u, rows)
    acc_ref[2] += dot_tn(inner, d_expert)
    acc_r_ref[...] += dot_tn(d_logits, rows)

    @pl.when(step == EXPERTS // SOURCES - 1)
    def _():
        out_r_ref[...] = acc_r_ref[...]
        if last:
            for place in range(SHARDS):
                shard = (mine_ref[1] + place) % SHARDS
                span = pl.ds(pl.multiple_of(shard * PIECE, PIECE), PIECE)
                rows = jnp.concatenate([acc_ref[which, span, :] for which in range(3)], axis=0)
                store_halves(place, rows.astype(BF16), out_refs)
        else:
            out_refs[0][...] = acc_ref[...]


def expert(part, mine, rows, cots, weights, w_router, carried):
    first, last, slots = part == 0, part == len(PARTS) - 1, PARTS[part]
    assert sum(PARTS[:part]) % slots == 0
    place = sum(PARTS[:part]) // slots
    block = (SOURCES, slots, WIDTH)
    y_rows = TOKENS if last else slots
    out_w = [jax.ShapeDtypeStruct((3, FF, WIDTH), F32)]
    if last:
        whole, half = (3 * PIECE, WIDTH), (3 * PIECE // 2, WIDTH)
        out_w = [jax.ShapeDtypeStruct(whole, BF16)] + [jax.ShapeDtypeStruct(half, BF16)] * 6
    return pl.pallas_call(
        functools.partial(expert_kernel, first, last, slots),
        grid=(EXPERTS // SOURCES,),
        in_specs=[
            pl.BlockSpec(memory_space=pltpu.SMEM),
            pl.BlockSpec(block, lambda i: (i, 0, 0)),
            pl.BlockSpec(block, lambda i: (i, place, 0)),
            fixed(weights.shape),
            fixed(w_router.shape),
        ]
        + [fixed(array.shape) for array in carried[:2]]
        + [pl.BlockSpec((SOURCES, TOKENS), lambda i: (i, 0)) for _ in carried[2:3]]
        + [pl.BlockSpec(block, lambda i: (i, 0, 0)) for _ in carried[3:]],
        out_specs=[
            pl.BlockSpec((SOURCES, y_rows, WIDTH), lambda i: (i, 0, 0)),
            pl.BlockSpec(block, lambda i: (i, 0, 0)),
            fixed((EXPERTS, WIDTH)),
        ]
        + [fixed(out.shape) for out in out_w],
        out_shape=[
            jax.ShapeDtypeStruct((EXPERTS, y_rows, WIDTH), BF16),
            jax.ShapeDtypeStruct((EXPERTS, slots, WIDTH), BF16),
            jax.ShapeDtypeStruct((EXPERTS, WIDTH), F32),
        ]
        + out_w,
        scratch_shapes=[
            pltpu.VMEM((WIDTH, FF), BF16),
            pltpu.VMEM((WIDTH, FF), BF16),
            pltpu.VMEM((WIDTH, FF), BF16),
            pltpu.VMEM((3, FF, WIDTH), F32),
            pltpu.VMEM((EXPERTS, WIDTH), F32),
        ],
        compiler_params=params(E_MIB),
        cost_estimate=cost(18 * EXPERTS * slots * WIDTH * FF, 8 * EXPERTS * slots * WIDTH),
        name="expert",
    )(mine, rows, cots, weights, w_router, *carried)


def exchange(rows):
    return lax.all_to_all(rows, "expert", split_axis=0, concat_axis=0, tiled=True)


RING = ([(0, 1), (1, 2), (2, 3), (3, 0)], [(1, 0), (2, 1), (3, 2), (0, 3)])


def to_right(rows):
    return lax.ppermute(rows, "shard", RING[0])


def to_left(rows):
    return lax.ppermute(rows, "shard", RING[1])


def ring_gather(top, bottom):
    left_top, right_bottom = to_right(top), to_left(bottom)
    left_bottom, right_top = to_right(bottom), to_left(top)
    far_top, far_bottom = to_right(left_top), to_left(right_bottom)
    return (top, bottom, right_top, right_bottom, far_top, far_bottom, left_top, left_bottom)


def ring_scatter(own, right_top, right_bottom, far_top, far_bottom, left_top, left_bottom):
    to_add_top, to_add_bottom = to_right(far_top), to_left(far_bottom)
    from_left_bottom, from_right_top = to_right(right_bottom), to_left(left_top)
    from_left_top = to_right(added(right_top, to_add_top))
    from_right_bottom = to_left(added(left_bottom, to_add_bottom))
    return (own, from_left_top, from_left_bottom, from_right_top, from_right_bottom)


def added(one, other):
    return (one.astype(F32) + other.astype(F32)).astype(BF16)


SAME_CORE = [[2 * chip + core for chip in range(CHIPS)] for core in range(2)]


def exchange_same_core(rows):
    return lax.all_to_all(
        rows, "expert", split_axis=0, concat_axis=0, tiled=True, axis_index_groups=SAME_CORE
    )


def partner_rows(values, axis, size, bit):
    return lax.ppermute(values, axis, [(index, index ^ bit) for index in range(size)])


def swap_cores(rows):
    return partner_rows(rows, "expert", EXPERTS, 1)


def over_column(values):
    values = values + swap_cores(values)
    far = partner_rows(values, "shard", SHARDS, 2)
    return (values + far) + (to_right(values) + to_left(values))


LATE = 3
SMALL = EXPERTS + LATE
SMALL_ROWS = -(-SMALL * (WIDTH // CHIPS) // QKV)
LOAD_ROWS = 64


def by_chip(small):
    return jnp.swapaxes(small.reshape(small.shape[0], CHIPS, -1), 0, 1).reshape(CHIPS, -1)


def pack_kernel(kept_ref, given_ref, small_ref, out_ref):
    first = ROWS_QKV + 2 * ROWS_OUT
    kept = kept_ref[...].astype(F32) + given_ref[...].astype(F32)
    out_ref[:, :first] = kept.astype(BF16)
    out_ref[:, first:] = three_pieces(small_ref[...], 1).astype(BF16)


def three_pieces(small, axis):
    high = small.astype(BF16).astype(F32)
    middle = (small - high).astype(BF16).astype(F32)
    low = small - high - middle
    rest = LOAD_ROWS - ROWS_QKV - 2 * ROWS_OUT - 3 * SMALL_ROWS
    blank = jnp.zeros_like(lax.slice_in_dim(small, 0, rest, axis=axis))
    return jnp.concatenate([high, middle, low, blank], axis=axis)


def pack(kept, given, small):
    out = jax.ShapeDtypeStruct((CHIPS, LOAD_ROWS, QKV), BF16)
    return pl.pallas_call(
        pack_kernel,
        grid=(1,),
        in_specs=[fixed(kept.shape), fixed(given.shape), fixed(small.shape)],
        out_specs=fixed(out.shape),
        out_shape=out,
        compiler_params=params(),
        cost_estimate=cost(0, 4 * MIB),
        name="pack",
    )(kept, given, small)


def add_kernel(pieces_ref, out_ref):
    first = ROWS_QKV + 2 * ROWS_OUT
    total = jnp.sum(pieces_ref[...].astype(F32), axis=0)
    small = total[first:]
    small = (
        small[:SMALL_ROWS] + small[SMALL_ROWS : 2 * SMALL_ROWS]
    ) + small[2 * SMALL_ROWS : 3 * SMALL_ROWS]
    rows = jnp.concatenate([total[:first], three_pieces(small, 0)], axis=0).astype(BF16)
    out_ref[...] = jnp.broadcast_to(rows[None], out_ref.shape)


def add_up(pieces):
    return pl.pallas_call(
        add_kernel,
        grid=(1,),
        in_specs=[fixed(pieces.shape)],
        out_specs=fixed(pieces.shape),
        out_shape=jax.ShapeDtypeStruct(pieces.shape, BF16),
        compiler_params=params(),
        cost_estimate=cost(0, 2 * MIB),
        name="add_up",
    )(pieces)


def after(value, *others):
    return lax.optimization_barrier((value, *others))[0]


def body(
    hidden_in, seq_lengths, routes, norm_gain1, w_query, w_key, w_value, query_gain, key_gain,
    w_out, norm_gain2, w_router, w_gate, w_up, w_down, cotangent,
):
    weights = jnp.stack([w_gate[0], w_up[0], w_down[0]], axis=0)
    routes_low = jnp.pad(routes.T.astype(BF16), ((0, 0), (0, WIDTH - TOKENS)))
    cots = lax.all_gather(jnp.concatenate([cotangent, routes_low], axis=0), "expert", axis=0)
    hidden_all = ring_gather(hidden_in[:HALF_ROWS], hidden_in[HALF_ROWS:])
    pick_first, place_first, pick_last, place_last = slot_tables(routes.T)

    lengths = seq_lengths[0]
    ends = jnp.cumsum(lengths)
    turn = lax.axis_index("shard").astype(jnp.int32) * TOKENS
    row_index = (jnp.arange(GROUP, dtype=jnp.int32) + turn) % GROUP
    segment = jnp.sum((row_index[:, None] >= ends[None, :]).astype(jnp.int32), axis=1)
    member = segment[:, None] == jnp.arange(lengths.shape[0], dtype=jnp.int32)[None, :]
    position = row_index - jnp.sum(jnp.where(member, (ends - lengths)[None, :], 0), axis=1)
    frequency = ROPE_BASE ** (-2.0 * jnp.arange(HALF, dtype=F32) / HEAD)
    angles = position.astype(F32)[:, None] * frequency[None, :]
    cosine, sine = jnp.cos(angles), jnp.sin(angles)
    cosine = jnp.concatenate([cosine] * 4, axis=1)
    sine = jnp.concatenate([-sine, sine] * 2, axis=1)
    feature_q = jnp.pad(member.astype(BF16), ((0, 0), (0, HEAD - 4)))
    feature_k = jnp.concatenate(
        [
            jnp.where(member, 0.0, -APART).astype(BF16),
            jnp.ones((GROUP, 3), BF16),
            jnp.zeros((GROUP, HEAD - 7), BF16),
        ],
        axis=1,
    )
    head_gain = jnp.concatenate([query_gain] * Q_HEADS + [key_gain] * K_HEADS)[None, :]
    gain1, gain2 = norm_gain1[None, :], norm_gain2[None, :]
    normed, raw_q, raw_k, keys, values, mixed, queries, *attended = attention(
        hidden_all, gain1, (w_query, w_key, w_value), head_gain, w_out, cosine, sine, feature_q, feature_k
    )
    attended = ring_scatter(*attended)
    weights = lax.all_gather(after(weights, *attended), "shard", axis=0)
    residual, rows, outgoing = norm2_dispatch(hidden_in, attended, gain2, pick_first)
    mine = jnp.stack([lax.axis_index("expert"), lax.axis_index("shard")]).astype(jnp.int32)
    arrived = [exchange(outgoing)]
    rows = after(rows, outgoing)
    cots, rank = collect(mine, after(cots, outgoing))
    normed_t = after(normed, outgoing).T
    w_qkv = jnp.concatenate(after((w_query, w_key, w_value), outgoing), axis=1)
    latest = exchange(after(dispatch(rows, pick_last), cots, normed_t))
    arrived.append(latest)
    carried, d_home = (), []
    for part, rows in enumerate(arrived):
        results, d_rows, d_r, *d_w = expert(part, mine, rows, cots, weights, w_router, carried)
        carried = (d_w[0], d_r, rank, results)
        latest = exchange(after(d_rows, latest))
        d_home.append(latest)
    d_router = d_r
    outputs = lax.psum_scatter(
        after(results, d_home[0]), "expert", scatter_dimension=0, tiled=False
    )

    d_experts = ring_scatter(*after(tuple(d_w), d_home[0]))
    d_router = over_column(after(d_router, d_home[0]))
    d_residual, d_top, d_bottom, gain2_share = norm2_back(
        residual, after(gain2, d_router, *d_experts), cotangent, (place_first, place_last), d_home
    )
    grads_all = ring_gather(d_top, d_bottom)
    core = mine[:1] % 2
    kept, given, head_share, gain1_share, *d_normed = attend_back(
        core, grads_all, normed, normed_t, gain1, w_qkv, w_out, queries, keys, values, mixed, raw_q, raw_k,
        head_gain, cosine, sine,
    )
    d_normed = ring_scatter(*d_normed)

    late = jnp.concatenate(
        [gain2_share, gain1_share, jnp.pad(head_share, ((0, 5), (0, WIDTH - QK)))], axis=0
    )
    small = jnp.concatenate([by_chip(d_router), by_chip(late[:LATE])], axis=1)
    small = jnp.pad(small, ((0, 0), (0, SMALL_ROWS * QKV - small.shape[1])))
    load = pack(kept, swap_cores(given), small.reshape(CHIPS, SMALL_ROWS, QKV))
    pieces = exchange_same_core(load)
    pieces = after(pieces, d_normed[2], d_normed[3])
    whole = exchange_same_core(add_up(pieces))
    grad_hidden = norm1_back(hidden_in, gain1, d_residual, d_normed)
    hidden_out = (residual + outputs.astype(F32)).astype(BF16)

    d_experts = turn_over(d_experts)
    whole = after(whole, hidden_out, grad_hidden, d_experts[0])
    grad_w_q, grad_w_k, grad_w_v, grad_w_out = widen(core, whole, swap_cores(whole))
    first = ROWS_QKV + 2 * ROWS_OUT
    small = whole[:, first : first + 3 * SMALL_ROWS].astype(F32)
    small = jnp.sum(small.reshape(CHIPS, 3, -1), axis=1)[:, : SMALL * (WIDTH // CHIPS)]
    small = jnp.swapaxes(small.reshape(CHIPS, SMALL, -1), 0, 1).reshape(SMALL, WIDTH)
    late = over_column(small[EXPERTS:])
    head_share = late[2]
    return (
        hidden_out,
        grad_hidden,
        late[1],
        grad_w_q,
        grad_w_k,
        grad_w_v,
        jnp.sum(head_share[:Q_LANES].reshape(Q_HEADS, HEAD), axis=0),
        jnp.sum(head_share[Q_LANES:QK].reshape(K_HEADS, HEAD), axis=0),
        grad_w_out,
        late[0],
        small[:EXPERTS].T,
        *d_experts,
    )


def solution(mesh):
    in_specs = (
        P(("expert", "shard"), None),
        P("expert", None),
        P(("expert", "shard"), None),
        P(),
        P(None, "shard"),
        P(None, "shard"),
        P(None, "shard"),
        P(),
        P(),
        P("shard", None),
        P(),
        P(),
        P("expert", None, "shard"),
        P("expert", None, "shard"),
        P("expert", None, "shard"),
        P(("expert", "shard"), None),
    )
    out_specs = (
        P(("expert", "shard"), None),
        P(("expert", "shard"), None),
        P(),
        P(None, "shard"),
        P(None, "shard"),
        P(None, "shard"),
        P(),
        P(),
        P("shard", None),
        P(),
        P(),
        P("expert", None, "shard"),
        P("expert", None, "shard"),
        P("expert", None, "shard"),
    )
    return jax.shard_map(body, mesh=mesh, in_specs=in_specs, out_specs=out_specs, check_vma=False)
```
